256 devices in a mesh: dp: 32 (over z, y), tensor: 8 (over x, core).
Axes of the slice: x: 4, y: 4, z: 8, core: 2. Of those that a mesh axis runs over, the one named last changes fastest.
Arguments:
- tokens: bfloat16 [4096, 8192], P('dp', 'tensor'), may hold values from -6 to 6
- gate_up: bfloat16 [8192, 2, 16384], P('tensor', None, 'dp'), may hold values from -0.0625 to 0.0625
- adapter_in: bfloat16 [32, 2, 16, 8192], P(None, None, None, 'tensor'), may hold values from -0.0625 to 0.0625
- adapter_out: bfloat16 [32, 2, 16, 16384], P(None, None, None, 'dp'), may hold values from -1.5 to 1.5
- d_hidden: bfloat16 [4096, 16384], P('tensor', 'dp'), may hold values from -0.1796875 to 0.1796875
- block_adapter: int32 [32], replicated, may hold values from 0 to 31
- block_live: int32 [32], replicated, may hold values from 1 to 128, as said below
- owner_slot: int32 [32], replicated, may hold values from 0 to 63, as said below
Outputs:
- hidden: bfloat16 [4096, 16384], P('tensor', 'dp')
- grad_in: float32 [64, 2, 16, 8192], P('dp', None, None, 'tensor')
- grad_out: float32 [64, 2, 16, 16384], P('dp', None, None, 'tensor')
The draws below stay inside these ranges and needn't reach their ends.
Inputs may be any that keep to these rules, and one draw needn't show every extreme that they name: `block_live`: block lengths; some block is full in every draw. `owner_slot`: distinct slots; slot s belongs to data group s // 2; some group holds 2 adapters in every draw.
All inputs are finite; a program needn't handle non-finite values.
Results may differ from the reference program's by a relative error of at most 0.0057.
Values may be sent and summed in bfloat16 or wider, within the bound.
No kernel may reach another device: no remote copies, remote signals or barrier semaphores. Data moves between devices by JAX's collectives and lax.ppermute only.
A program may use at most 128 MiB of HBM per device.

```python
import math
import jax
import jax.numpy as jnp
import numpy as np
from jax import lax

D = 8192
HIDDEN_SLICE = 16384
R = 16
ADAPTERS = 32
BLOCK_ROWS = 128
TOKENS = 4096
BLOCK_COUNT = 32
SLOTS = 64
OWN = 2


def draw_block_live(key, part):
    key = jax.random.fold_in(key, 11)
    first_key, second_key = jax.random.split(key)
    lengths = jax.random.randint(first_key, (BLOCK_COUNT,), 1, BLOCK_ROWS + 1)
    chosen = jax.random.randint(second_key, (), 0, BLOCK_COUNT)
    return jnp.where(jnp.arange(BLOCK_COUNT) == chosen, BLOCK_ROWS, lengths).astype(jnp.int32)


def draw_owner_slot(key, part):
    key = jax.random.fold_in(key, 23)
    first_key, second_key = jax.random.split(key)
    shuffled = jax.random.permutation(first_key, SLOTS).astype(jnp.int32)
    full_group = jax.random.randint(second_key, (), 0, SLOTS // OWN)
    ranking = (shuffled // OWN != full_group).astype(jnp.int32)
    ordered = shuffled[jnp.argsort(ranking, stable=True)]
    return ordered[:ADAPTERS].astype(jnp.int32)


def place_ends(result, rng, smallest, high):
    extent = result.shape
    place = [jax.random.randint(jax.random.fold_in(rng, axis), (), 0, extent[axis]) for axis in range(len(extent))]
    result = result.at[tuple(place)].set(smallest)
    longest = extent.index(max(extent))
    place[longest] = (place[longest] + 1) % extent[longest]
    return result.at[tuple(place)].set(high)


def levels(own_key, extent, shards, least, largest):
    level = 1.0
    for dim, blocks in shards:
        draws = jax.random.uniform(jax.random.fold_in(jax.random.fold_in(own_key, 6), dim), (blocks,), jnp.float32, least / len(shards), largest / len(shards))
        level = level * jnp.repeat(jnp.exp(draws), extent[dim] // blocks).reshape((-1,) + (1,) * (len(extent) - 1 - dim))
    return level


def cumulative_ranks(amount, skew):
    portions = [(1 << 20) // math.isqrt(standing ** skew) + 1 for standing in range(1, amount + 1)]
    width = 1 + sum(portions) // (1 << 30)
    return np.cumsum(np.array([max(1, weight // width) for weight in portions]))


def ranked_ids(key, extent, count, lean):
    listing = cumulative_ranks(count, lean)
    pick = jax.random.randint(jax.random.fold_in(key, 1), extent, 0, int(listing[count - 1]))
    standing = jnp.searchsorted(jnp.asarray(listing, jnp.int32), pick, side="right")
    return jax.random.permutation(jax.random.fold_in(key, 2), count)[standing].astype(jnp.int32)


def scatter_about(rng, dims, spread, bound, cuts=(), kind=jnp.bfloat16):
    array = spread * jax.random.normal(rng, dims, jnp.float32)
    if cuts:
        array = array * levels(rng, dims, cuts, -0.22, 0.18)
    return jnp.clip(array, -bound, bound).astype(kind)


def setup_inputs(seed: int = 0) -> dict:
    arg_keys = jax.random.split(jax.random.key(seed), 9)
    return {
        "tokens": scatter_about(arg_keys[0], (TOKENS, D), 1.0, 6.0, ((0, 32), (1, 8))),
        "gate_up": scatter_about(arg_keys[1], (D, 2, HIDDEN_SLICE), D ** -0.5, 0.0625, ((0, 8), (2, 32))),
        "adapter_in": scatter_about(arg_keys[2], (ADAPTERS, 2, R, D), D ** -0.5, 0.0625, ((3, 8),)),
        "adapter_out": scatter_about(arg_keys[3], (ADAPTERS, 2, R, HIDDEN_SLICE), R ** -0.5, 1.5, ((3, 32),)),
        "d_hidden": scatter_about(arg_keys[4], (TOKENS, HIDDEN_SLICE), 0.03, 0.1796875, ((0, 8), (1, 32))),
        "block_adapter": place_ends(ranked_ids(arg_keys[5], (BLOCK_COUNT,), ADAPTERS, 2), jax.random.fold_in(arg_keys[5], 3), 0, ADAPTERS - 1).astype(jnp.int32),
        "block_live": draw_block_live(jax.random.fold_in(arg_keys[8], 71), 0),
        "owner_slot": draw_owner_slot(jax.random.fold_in(arg_keys[8], 71), 0),
    }


def reference(tokens, gate_up, adapter_in, adapter_out, d_hidden, block_adapter, block_live, owner_slot):
    weights = gate_up.reshape(D, 2 * HIDDEN_SLICE)
    base_output = jnp.dot(tokens, weights, preferred_element_type=jnp.float32)
    in_sel = adapter_in[block_adapter].astype(jnp.float32)
    output_selector = adapter_out[block_adapter].astype(jnp.float32)
    row_blocks = tokens.reshape(BLOCK_COUNT, BLOCK_ROWS, D).astype(jnp.float32)
    rank_state = jnp.einsum('brd,bgkd->brgk', row_blocks, in_sel).astype(jnp.bfloat16)
    adapter_output = jnp.einsum('iacz,iczs->iacs', rank_state.astype(jnp.float32), output_selector)
    gate_input = base_output.reshape(BLOCK_COUNT, BLOCK_ROWS, 2, HIDDEN_SLICE) + adapter_output
    gate = gate_input[:, :, 0]
    up_part = gate_input[:, :, 1]
    hidden = (jax.nn.silu(gate) * up_part).astype(jnp.bfloat16).reshape(TOKENS, HIDDEN_SLICE)
    live = (jnp.arange(BLOCK_ROWS, dtype=jnp.int32)[None, :] < block_live[:, None]).astype(jnp.float32)
    cotan = d_hidden.reshape(BLOCK_COUNT, BLOCK_ROWS, HIDDEN_SLICE).astype(jnp.float32) * live[:, :, None]
    sigma = jax.nn.sigmoid(gate)
    dgate = cotan * up_part * sigma * (1.0 + gate * (1.0 - sigma))
    dup = cotan * gate * sigma
    dpre = jnp.stack([dgate, dup], 2).astype(jnp.bfloat16)
    dlow = jnp.einsum('brgf,bgkf->brgk', dpre.astype(jnp.float32), output_selector).astype(jnp.bfloat16)
    block_in = jnp.einsum('brgk,brd->bgkd', dlow.astype(jnp.float32), row_blocks)
    block_out = jnp.einsum('brgk,brgf->bgkf', rank_state.astype(jnp.float32), dpre.astype(jnp.float32))
    slot_of = owner_slot[block_adapter]
    picker = (jnp.arange(SLOTS, dtype=jnp.int32)[:, None] == slot_of[None, :]).astype(jnp.float32)
    grad_in = jnp.einsum('sb,bgkd->sgkd', picker, block_in, precision=lax.Precision.HIGHEST)
    grad_out = jnp.einsum('sb,bgkf->sgkf', picker, block_out, precision=lax.Precision.HIGHEST)
    return hidden, grad_in, grad_out
```

```python
import jax
import jax.numpy as jnp
from jax import lax
from jax.experimental import pallas as pl
from jax.experimental.pallas import tpu as pltpu
from jax.sharding import PartitionSpec as P

R = 16
RANKS = 2 * R
BLOCK_ROWS = 128
Z, Y, X, C = 8, 4, 4, 2
N_DP, N_TENSOR = Z * Y, X * C
OWN = 2
SLOTS = OWN * N_DP
BF16, F32 = jnp.bfloat16, jnp.float32

SWAP = [((z * Y + y) * N_TENSOR + t, (t * Y + y) * N_TENSOR + z)
        for z in range(Z) for y in range(Y) for t in range(N_TENSOR)]


def shift_x(step):
    return [(x * C + c, ((x + step) % X) * C + c) for x in range(X) for c in range(C)]


SIBLING = [(x * C + c, x * C + 1 - c) for x in range(X) for c in range(C)]


def gather_weights(own):
    half = own.shape[0] // 2
    x, c = lax.axis_index("tensor") // C, lax.axis_index("tensor") % C
    left = lax.ppermute(own, "tensor", shift_x(1))
    right = lax.ppermute(own, "tensor", shift_x(-1))
    far_a = lax.ppermute(left[:half], "tensor", shift_x(1))
    far_b = lax.ppermute(right[half:], "tensor", shift_x(-1))
    pieces = [(0, 0, own), (1, 0, left), (3, 0, right), (2, 0, far_a), (2, half, far_b)]
    full = jnp.zeros((N_TENSOR,) + own.shape, own.dtype)
    for back, row, piece in pieces:
        place = ((x - back) % X) * C
        other = lax.ppermute(piece, "tensor", SIBLING)
        full = lax.dynamic_update_slice(full, piece[None], (place + c, row, 0))
        full = lax.dynamic_update_slice(full, other[None], (place + 1 - c, row, 0))
    return full


def block_kernel(live_ref, x_ref, w_ref, low_ref, out_map_ref, cot_ref,
                 hidden_ref, dlow_ref, grad_ref, acc_ref):
    k = pl.program_id(0)
    part = jnp.dot(x_ref[0], w_ref[0], preferred_element_type=F32)

    @pl.when(k == 0)
    def _():
        acc_ref[...] = part

    @pl.when(k > 0)
    def _():
        acc_ref[...] += part

    @pl.when(k == pl.num_programs(0) - 1)
    def _():
        half = cot_ref.shape[1]
        for b in range(acc_ref.shape[0] // BLOCK_ROWS):
            rows = slice(b * BLOCK_ROWS, (b + 1) * BLOCK_ROWS)
            ranks = slice(b * RANKS, (b + 1) * RANKS)
            low = low_ref[ranks, :]
            out_map = out_map_ref[b]
            pre = acc_ref[rows, :] + lax.dot_general(
                low, out_map, (((0,), (0,)), ((), ())), preferred_element_type=F32)
            gate, up = pre[:, :half], pre[:, half:]
            sigma = jax.nn.sigmoid(gate)
            gated = gate * sigma
            hidden_ref[rows, :] = (gated * up).astype(BF16)
            live = lax.broadcasted_iota(jnp.int32, (BLOCK_ROWS, half), 0) < live_ref[b]
            cotan = jnp.where(live, cot_ref[rows, :].astype(F32), 0.0)
            dgate = cotan * up * sigma * (1.0 + gate * (1.0 - sigma))
            dup = cotan * gated
            dpre = jnp.concatenate([dgate, dup], 1).astype(BF16)
            dlow_ref[ranks, :] = lax.dot_general(
                out_map, dpre, (((1,), (1,)), ((), ())), preferred_element_type=F32)
            grad = jnp.dot(low, dpre, preferred_element_type=F32)
            grad_ref[b, :R, :] = grad[:R, :half]
            grad_ref[b, R:, :] = grad[R:, half:]


def project(live, rows, weights, low, out_map, cotan):
    parts, n_rows, depth = rows.shape
    width = weights.shape[2]
    blocks = n_rows // BLOCK_ROWS
    half = width // 2
    return pl.pallas_call(
        block_kernel,
        grid_spec=pltpu.PrefetchScalarGridSpec(
            num_scalar_prefetch=1,
            grid=(parts,),
            in_specs=[
                pl.BlockSpec((1, n_rows, depth), lambda k, s: (k, 0, 0)),
                pl.BlockSpec((1, depth, width), lambda k, s: (k, 0, 0)),
                pl.BlockSpec(low.shape, lambda k, s: (0, 0)),
                pl.BlockSpec(out_map.shape, lambda k, s: (0, 0, 0)),
                pl.BlockSpec(cotan.shape, lambda k, s: (0, 0)),
            ],
            out_specs=[
                pl.BlockSpec((n_rows, half), lambda k, s: (0, 0)),
                pl.BlockSpec(low.shape, lambda k, s: (0, 0)),
                pl.BlockSpec((blocks, RANKS, half), lambda k, s: (0, 0, 0)),
            ],
            scratch_shapes=[pltpu.VMEM((n_rows, width), F32)],
        ),
        out_shape=[
            jax.ShapeDtypeStruct((n_rows, half), BF16),
            jax.ShapeDtypeStruct(low.shape, F32),
            jax.ShapeDtypeStruct((blocks, RANKS, half), F32),
        ],
        compiler_params=pltpu.CompilerParams(vmem_limit_bytes=40 * 2 ** 20),
        cost_estimate=pl.CostEstimate(
            flops=2 * parts * n_rows * depth * width,
            bytes_accessed=2 * parts * depth * (n_rows + width),
            transcendentals=n_rows * half),
    )(live, rows, weights, low, out_map, cotan)


def body(tokens, gate_up, adapter_in, adapter_out, d_hidden, block_adapter, block_live, owner_slot):
    dp, tensor = lax.axis_index("dp"), lax.axis_index("tensor")
    d_part, hidden_part = tokens.shape[1], gate_up.shape[2]
    blocks = d_hidden.shape[0] // BLOCK_ROWS
    n_rows = blocks * BLOCK_ROWS
    lanes = RANKS * blocks

    swapped = lax.ppermute(tokens, ("dp", "tensor"), SWAP)
    rows = lax.all_gather(swapped, "dp", axis=0, tiled=True).reshape(Z, n_rows, d_part)
    weights = gather_weights(gate_up.reshape(d_part, 2 * hidden_part))

    in_map = lax.dynamic_index_in_dim(adapter_in, block_adapter[dp], 0, False).reshape(RANKS, d_part)
    low_part = lax.dot_general(in_map, tokens, (((1,), (1,)), ((), ())), preferred_element_type=F32)
    per = RANKS // N_TENSOR
    low_sum = lax.all_to_all(low_part.reshape(N_TENSOR, per, BLOCK_ROWS), "tensor", 0, 0, tiled=True).sum(0)
    low_own = lax.ppermute(low_sum.astype(BF16), ("dp", "tensor"), SWAP)
    low = lax.all_to_all(jnp.broadcast_to(low_own[None], (N_DP,) + low_own.shape), "dp", 0, 0, tiled=True)
    low = low.reshape(Z, blocks, per, BLOCK_ROWS).transpose(1, 0, 2, 3).reshape(lanes, BLOCK_ROWS)

    local_ids = lax.dynamic_slice_in_dim(block_adapter, tensor * blocks, blocks, 0)
    local_live = lax.dynamic_slice_in_dim(block_live, tensor * blocks, blocks, 0)
    picked = adapter_out[local_ids]
    out_map = jnp.concatenate([
        jnp.pad(picked[:, 0], ((0, 0), (0, 0), (0, hidden_part))),
        jnp.pad(picked[:, 1], ((0, 0), (0, 0), (hidden_part, 0)))], 1)

    hidden, dlow_part, block_grad = project(local_live, rows, weights, low, out_map, d_hidden)

    shared = lax.all_to_all(
        block_grad.astype(BF16).reshape(blocks, N_TENSOR, per, hidden_part).transpose(1, 0, 2, 3),
        "tensor", 0, 0, tiled=True).reshape(N_TENSOR * blocks, per * hidden_part)
    slot_of = owner_slot[block_adapter]
    picker = (jnp.arange(SLOTS, dtype=jnp.int32)[:, None] == slot_of[None, :]).astype(BF16)
    slotted = jnp.dot(picker, shared, preferred_element_type=F32).astype(BF16)

    local_slot = lax.dynamic_slice_in_dim(slot_of, tensor * blocks, blocks, 0)
    owner = jnp.repeat(local_slot // OWN, RANKS)
    owned = jnp.arange(N_DP, dtype=jnp.int32)[:, None] == owner[None, :]
    dlow_out = jnp.where(owned[:, :, None], dlow_part.astype(BF16)[None], jnp.zeros((), BF16))
    n_slot = OWN * per * hidden_part // BLOCK_ROWS
    sent = jnp.concatenate([slotted.reshape(N_DP, n_slot, BLOCK_ROWS), dlow_out], 1)
    got = lax.all_to_all(sent, "dp", 0, 0, tiled=True)
    dlow = got[:, n_slot:].astype(F32).sum(0)

    mine = (jnp.arange(OWN, dtype=jnp.int32)[:, None] + OWN * dp == local_slot[None, :])
    weighted = jnp.where(mine[:, None, :, None], dlow.reshape(blocks, RANKS, BLOCK_ROWS).transpose(1, 0, 2)[None], 0.0)
    weighted = weighted.reshape(OWN * RANKS, n_rows).astype(BF16)
    in_part = jnp.einsum("mr,zrk->zmk", weighted, rows, preferred_element_type=F32).astype(BF16)

    out_part = got[:, :n_slot].reshape(N_TENSOR, -1, d_part)
    n_in = OWN * RANKS
    last = lax.all_to_all(jnp.concatenate([in_part, out_part], 1), "tensor", 0, 0, tiled=True)
    grad_in = last[:, :n_in].astype(F32).sum(0).reshape(OWN, 2, R, d_part)
    grad_out = last[:, n_in:].reshape(N_TENSOR, Y, OWN, per, hidden_part).transpose(2, 0, 3, 1, 4)
    grad_out = grad_out.reshape(OWN, 2, R, Y * hidden_part).astype(F32)
    return hidden, grad_in, grad_out


def solution(mesh):
    placed = (
        P("dp", "tensor"),
        P("tensor", None, "dp"),
        P(None, None, None, "tensor"),
        P(None, None, None, "dp"),
        P("tensor", "dp"),
        P(),
        P(),
        P(),
    )
    return jax.shard_map(
        body,
        mesh=mesh,
        in_specs=placed,
        out_specs=(P("tensor", "dp"), P("dp", None, None, "tensor"), P("dp", None, None, "tensor")),
        check_vma=False,
    )
```

```python
import jax
import jax.numpy as jnp
from jax import lax
from jax.experimental import pallas as pl
from jax.experimental.pallas import tpu as pltpu
from jax.sharding import Mesh, PartitionSpec as P

R = 16
RANKS = 2 * R
BLOCK_ROWS = 128
HEAD = 64
Z, Y, X, C = 8, 4, 4, 2
N_DP, N_TENSOR = Z * Y, X * C
OWN = 2
SLOTS = OWN * N_DP
DP, TENSOR = ("z", "y"), ("x", "c")
BF16, F32 = jnp.bfloat16, jnp.float32
VMEM_LIMIT = 48 * 2 ** 20


def swap(skew):
    return [((z * Y + y) * N_TENSOR + t, (((t + skew * z) % Z) * Y + y) * N_TENSOR + z)
            for z in range(Z) for y in range(Y) for t in range(N_TENSOR)]


def exchange(x, axes):
    return lax.all_to_all(x, axes, 0, 0, tiled=True)


def spread(x, axis, n):
    return exchange(jnp.broadcast_to(x[None], (n,) + x.shape), axis)


def ring(x, axis, n):
    def send(v, step):
        return lax.ppermute(v, axis, [(i, (i + step) % n) for i in range(n)])

    half = x.shape[0] // 2
    pieces, up, down = [(0, None, x)], x, x
    for back in range(1, n // 2):
        up, down = send(up, 1), send(down, -1)
        pieces += [(back, None, up), (n - back, None, down)]
    return pieces + [(n // 2, 0, send(up[:half], 1)), (n // 2, 1, send(down[half:], -1))]


def block_kernel(n_head, heads, tails, where_ref, *refs):
    pieces, refs = refs[:len(heads) + len(tails)], refs[len(heads) + len(tails):]
    (w_ref, low_ref, out_map_ref, cot_ref, rows_ref, hidden_ref, dlow_ref, grad_ref,
     x_buf, w_buf, acc_ref, x_sem, w_sem, out_sem) = refs
    parts, blocks, _, depth = x_buf.shape
    z, y, t = where_ref[0], where_ref[1], where_ref[2]

    def feature(k):
        return lax.rem(k - t + parts, parts)

    loads = []
    for i, (back, part) in enumerate(heads):
        at = lax.rem(z - back + parts, parts)
        span = slice(0, blocks) if part is None else slice(part * blocks // 2, (part + 1) * blocks // 2)
        loads.append((pieces[i], x_buf.at[at, span, pl.ds(0, n_head)]))
    for i, (back, part) in enumerate(tails):
        at = lax.rem(y - back + blocks, blocks)
        span = slice(0, parts) if part is None else slice(part * parts // 2, (part + 1) * parts // 2)
        loads.append((pieces[len(heads) + i], x_buf.at[span, at, pl.ds(n_head, BLOCK_ROWS - n_head)]))
    loads = [pltpu.make_async_copy(src, dst, x_sem.at[i]) for i, (src, dst) in enumerate(loads)]
    for load in loads:
        load.start()

    def weight(k):
        return pltpu.make_async_copy(w_ref.at[feature(k)], w_buf.at[k], w_sem.at[k])

    def keep(k):
        return pltpu.make_async_copy(x_buf.at[k], rows_ref.at[feature(k)], out_sem.at[k])

    @pl.loop(0, parts)
    def _(k):
        weight(k).start()

    acc_ref[...] = jnp.zeros_like(acc_ref)
    for load in loads:
        load.wait()

    @pl.loop(0, parts)
    def _(k):
        weight(k).wait()
        keep(k).start()
        rows = x_buf[k].reshape(blocks * BLOCK_ROWS, depth)
        acc_ref[...] += jnp.dot(rows, w_buf[k], preferred_element_type=F32)

    half = cot_ref.shape[1]
    for b in range(blocks):
        rows = slice(b * BLOCK_ROWS, (b + 1) * BLOCK_ROWS)
        ranks = slice(b * RANKS, (b + 1) * RANKS)
        low = low_ref[ranks, :]
        out_map = out_map_ref[b]
        pre = acc_ref[rows, :] + lax.dot_general(
            low, out_map, (((0,), (0,)), ((), ())), preferred_element_type=F32)
        gate, up = pre[:, :half], pre[:, half:]
        sigma = jax.nn.sigmoid(gate)
        gated = gate * sigma
        hidden_ref[rows, :] = (gated * up).astype(BF16)
        live = lax.broadcasted_iota(jnp.int32, (BLOCK_ROWS, half), 0) < where_ref[3 + b]
        cotan = jnp.where(live, cot_ref[rows, :].astype(F32), 0.0)
        dgate = cotan * up * sigma * (1.0 + gate * (1.0 - sigma))
        dup = cotan * gated
        dpre = jnp.concatenate([dgate, dup], 1).astype(BF16)
        dlow_ref[ranks, :] = lax.dot_general(
            out_map, dpre, (((1,), (1,)), ((), ())), preferred_element_type=F32)
        grad = jnp.dot(low, dpre, preferred_element_type=F32)
        grad_ref[b, :R, :] = grad[:R, :half].astype(BF16)
        grad_ref[b, R:, :] = grad[R:, half:].astype(BF16)

    @pl.loop(0, parts)
    def _(k):
        keep(k).wait()


def project(where, heads, tails, weights, low, out_map, cotan):
    parts, depth, width = weights.shape
    n_rows, half = cotan.shape
    blocks = n_rows // BLOCK_ROWS
    n_head = heads[0][2].shape[-2]
    any_spec = pl.BlockSpec(memory_space=pl.ANY)
    vmem_spec = pl.BlockSpec(memory_space=pltpu.VMEM)
    n_pieces = len(heads) + len(tails)

    def kernel(*refs):
        block_kernel(n_head, [h[:2] for h in heads], [t[:2] for t in tails], *refs)

    return pl.pallas_call(
        kernel,
        in_specs=[pl.BlockSpec(memory_space=pltpu.SMEM)] + [any_spec] * (n_pieces + 1) + [vmem_spec] * 3,
        out_specs=[any_spec, vmem_spec, vmem_spec, vmem_spec],
        out_shape=[
            jax.ShapeDtypeStruct((parts, blocks, BLOCK_ROWS, depth), BF16),
            jax.ShapeDtypeStruct((n_rows, half), BF16),
            jax.ShapeDtypeStruct(low.shape, F32),
            jax.ShapeDtypeStruct((blocks, RANKS, half), BF16),
        ],
        scratch_shapes=[
            pltpu.VMEM((parts, blocks, BLOCK_ROWS, depth), BF16),
            pltpu.VMEM((parts, depth, width), BF16),
            pltpu.VMEM((n_rows, width), F32),
            pltpu.SemaphoreType.DMA((n_pieces,)),
            pltpu.SemaphoreType.DMA((parts,)),
            pltpu.SemaphoreType.DMA((parts,)),
        ],
        compiler_params=pltpu.CompilerParams(vmem_limit_bytes=VMEM_LIMIT),
        cost_estimate=pl.CostEstimate(
            flops=2 * parts * n_rows * depth * width,
            bytes_accessed=2 * parts * depth * (2 * n_rows + width),
            transcendentals=n_rows * half),
    )(where, *[h[2] for h in heads], *[t[2] for t in tails], weights, low, out_map, cotan)


def in_grad_kernel(mine_ref, dlow_ref, rows_ref, out_ref, left_ref):
    blocks = rows_ref.shape[1]

    @pl.when(pl.program_id(0) == 0)
    def _():
        for s in range(OWN):
            for b in range(blocks):
                picked = dlow_ref[b * RANKS:(b + 1) * RANKS, :].astype(F32)
                picked = jnp.where(mine_ref[s * blocks + b] == 1, picked, 0.0)
                left_ref[s * RANKS:(s + 1) * RANKS, b * BLOCK_ROWS:(b + 1) * BLOCK_ROWS] = picked.astype(BF16)

    rows = rows_ref[0].reshape(blocks * BLOCK_ROWS, rows_ref.shape[3])
    out_ref[0] = jnp.dot(left_ref[...], rows, preferred_element_type=F32).astype(BF16)


def in_grad(mine, dlow, rows):
    parts, blocks, _, depth = rows.shape
    n_out, n_rows = OWN * RANKS, blocks * BLOCK_ROWS
    return pl.pallas_call(
        in_grad_kernel,
        grid_spec=pltpu.PrefetchScalarGridSpec(
            num_scalar_prefetch=1,
            grid=(parts,),
            in_specs=[
                pl.BlockSpec(dlow.shape, lambda k, s: (0, 0)),
                pl.BlockSpec((1,) + rows.shape[1:], lambda k, s: (k, 0, 0, 0)),
            ],
            out_specs=pl.BlockSpec((1, n_out, depth), lambda k, s: (k, 0, 0)),
            scratch_shapes=[pltpu.VMEM((n_out, n_rows), BF16)],
        ),
        out_shape=jax.ShapeDtypeStruct((parts, n_out, depth), BF16),
        compiler_params=pltpu.CompilerParams(vmem_limit_bytes=VMEM_LIMIT),
        cost_estimate=pl.CostEstimate(
            flops=2 * parts * n_out * n_rows * depth,
            bytes_accessed=2 * parts * depth * (n_rows + n_out), transcendentals=0),
    )(mine, dlow, rows)


def out_grad_kernel(got_ref, out_ref):
    parts, quarters, _, width = got_ref.shape
    per = RANKS // parts
    for p in range(parts):
        for q in range(quarters):
            piece = got_ref[p, q].astype(F32)
            for s in range(OWN):
                out_ref[s, p * per:(p + 1) * per, q * width:(q + 1) * width] = piece[s * per:(s + 1) * per]


def body(tokens, gate_up, adapter_in, adapter_out, d_hidden, block_adapter, block_live, owner_slot):
    z, y = lax.axis_index("z"), lax.axis_index("y")
    dp, tensor = lax.axis_index(DP), lax.axis_index(TENSOR)
    d_part, hidden_part = tokens.shape[1], gate_up.shape[2]
    blocks = d_hidden.shape[0] // BLOCK_ROWS
    lanes = RANKS * blocks
    per = RANKS // N_TENSOR

    weights = lax.all_gather(gate_up.reshape(d_part, 2 * hidden_part), TENSOR, axis=0, tiled=False)

    swapped = lax.ppermute(tokens, DP + TENSOR, swap(1))
    heads = ring(spread(swapped[:HEAD], "y", Y), "z", Z)
    tails = ring(spread(swapped[HEAD:], "z", Z), "y", Y)

    in_map = lax.dynamic_index_in_dim(adapter_in, block_adapter[dp], 0, False).reshape(RANKS, d_part)
    low_part = lax.dot_general(in_map, tokens, (((1,), (1,)), ((), ())), preferred_element_type=F32)
    low_sum = exchange(low_part.reshape(N_TENSOR, per, BLOCK_ROWS), TENSOR).sum(0)
    low_own = lax.ppermute(low_sum.astype(BF16), DP + TENSOR, swap(0))
    low = spread(low_own, DP, N_DP).reshape(Z, Y, per, BLOCK_ROWS)
    low = low.transpose(1, 0, 2, 3).reshape(lanes, BLOCK_ROWS)

    local_ids = lax.dynamic_slice_in_dim(block_adapter, tensor * blocks, blocks, 0)
    local_live = lax.dynamic_slice_in_dim(block_live, tensor * blocks, blocks, 0)
    picked = adapter_out[local_ids]
    out_map = jnp.concatenate([
        jnp.pad(picked[:, 0], ((0, 0), (0, 0), (0, hidden_part))),
        jnp.pad(picked[:, 1], ((0, 0), (0, 0), (hidden_part, 0)))], 1)
    where = jnp.concatenate([jnp.stack([z, y, tensor]).astype(jnp.int32), local_live])

    rows, hidden, dlow_part, block_grad = project(where, heads, tails, weights, low, out_map, d_hidden)

    slot_of = owner_slot[block_adapter]
    local_slot = lax.dynamic_slice_in_dim(slot_of, tensor * blocks, blocks, 0)
    mine = jnp.arange(OWN, dtype=jnp.int32)[:, None] + OWN * dp == local_slot[None, :]

    dlow_sum = exchange(dlow_part.reshape(N_DP, lanes // N_DP, BLOCK_ROWS), DP).sum(0).astype(BF16)
    dlow = spread(dlow_sum, DP, N_DP).reshape(lanes, BLOCK_ROWS)
    in_part = in_grad(mine.reshape(-1).astype(jnp.int32), dlow, rows)
    grad_in = exchange(in_part, TENSOR).astype(F32).sum(0).reshape(OWN, 2, R, d_part)

    shared = exchange(
        block_grad.reshape(blocks, N_TENSOR, per, hidden_part).transpose(1, 0, 2, 3), TENSOR)
    picker = (jnp.arange(SLOTS, dtype=jnp.int32)[:, None] == slot_of[None, :]).astype(BF16)
    slotted = jnp.dot(picker, shared.reshape(N_TENSOR * blocks, per * hidden_part), preferred_element_type=F32)
    got = exchange(slotted.astype(BF16).reshape(N_DP, OWN * per, hidden_part), DP)
    got = exchange(got.reshape(N_TENSOR, Y, OWN * per, hidden_part), TENSOR)
    grad_out = pl.pallas_call(
        out_grad_kernel,
        out_shape=jax.ShapeDtypeStruct((OWN, RANKS, Y * hidden_part), F32),
    )(got).reshape(OWN, 2, R, Y * hidden_part)
    return hidden, grad_in, grad_out


def solution(mesh):
    mesh = Mesh(mesh.devices.reshape(Z, Y, X, C), DP + TENSOR)

    return jax.shard_map(
        body,
        mesh=mesh,
        in_specs=(P(DP, TENSOR), P(TENSOR, None, DP), P(None, None, None, TENSOR), P(None, None, None, DP),
                  P(TENSOR, DP), P(), P(), P()),
        out_specs=(P(TENSOR, DP), P(DP, None, None, TENSOR), P(DP, None, None, TENSOR)),
        check_vma=False,
    )
```

```python
import jax
import jax.numpy as jnp
from jax import lax
from jax.experimental import pallas as pl
from jax.experimental.pallas import tpu as pltpu
from jax.sharding import Mesh, PartitionSpec as P

R = 16
RANKS = 2 * R
BLOCK_ROWS = 128
Z, Y, X, C = 8, 4, 4, 2
N_DP, N_TENSOR = Z * Y, X * C
OWN = 2
SLOTS = OWN * N_DP
DP, TENSOR = ("z", "y"), ("x", "c")
BF16, F32 = jnp.bfloat16, jnp.float32
VMEM_LIMIT = 48 * 2 ** 20


def swap(skew):
    return [((z * Y + y) * N_TENSOR + t, (((t + skew * z) % Z) * Y + y) * N_TENSOR + z)
            for z in range(Z) for y in range(Y) for t in range(N_TENSOR)]


def exchange(x, axes):
    return lax.all_to_all(x, axes, 0, 0, tiled=True)


def spread(x, axis, n):
    return exchange(jnp.broadcast_to(x[None], (n,) + x.shape), axis)


def hop(x, axis, n, step):
    return lax.ppermute(x, axis, [(i, (i + step) % n) for i in range(n)])


def last_hop(up, down, axis, n):
    pairs = []
    for i in range(n):
        for c in range(C):
            pairs.append((i * C + c, ((i + (1 if c == 0 else -1)) % n) * C + c))
    return lax.ppermute(jnp.where(lax.axis_index("c") == 0, up, down), (axis, "c"), pairs)


def block_kernel(where_ref, rows_ref, *refs):
    weights, refs = refs[:N_TENSOR], refs[N_TENSOR:]
    low_ref, out_map_ref, cot_ref, hidden_ref, sent_ref, x_buf, w_buf, acc_ref, x_sem, w_sem = refs
    parts, blocks, _, depth = x_buf.shape
    t = where_ref[0]

    def place(i):
        x, c = lax.div(t, C), lax.rem(t, C)
        step, other = lax.div(i, C), lax.rem(i, C)
        back = jnp.where(step < 2, step, 5 - step)
        feature = lax.rem(x - back + X, X) * C + lax.rem(c + other, C)
        return lax.rem(feature + t, parts)

    def load(i):
        return pltpu.make_async_copy(rows_ref.at[place(i)], x_buf.at[i], x_sem.at[i])

    for i, weight in enumerate(weights):
        load(i).start()
        pltpu.make_async_copy(weight, w_buf.at[i], w_sem.at[i]).start()
    acc_ref[...] = jnp.zeros_like(acc_ref)

    @pl.loop(0, parts)
    def _(i):
        load(i).wait()
        pltpu.make_async_copy(w_buf.at[i], w_buf.at[i], w_sem.at[i]).wait()
        rows = x_buf[i].reshape(blocks * BLOCK_ROWS, depth)
        acc_ref[...] += jnp.dot(rows, w_buf[i], preferred_element_type=F32)

    half = cot_ref.shape[1]
    for b in range(blocks):
        rows = slice(b * BLOCK_ROWS, (b + 1) * BLOCK_ROWS)
        ranks = slice(b * RANKS, (b + 1) * RANKS)
        low = low_ref[ranks, :]
        out_map = out_map_ref[b]
        pre = acc_ref[rows, :] + lax.dot_general(
            low, out_map, (((0,), (0,)), ((), ())), preferred_element_type=F32)
        gate, up = pre[:, :half], pre[:, half:]
        sigma = jax.nn.sigmoid(gate)
        gated = gate * sigma
        hidden_ref[rows, :] = (gated * up).astype(BF16)
        live = lax.broadcasted_iota(jnp.int32, (BLOCK_ROWS, half), 0) < where_ref[1 + b]
        cotan = jnp.where(live, cot_ref[rows, :].astype(F32), 0.0)
        dgate = cotan * up * sigma * (1.0 + gate * (1.0 - sigma))
        dup = cotan * gated
        dpre = jnp.concatenate([dgate, dup], 1).astype(BF16)
        grad = jnp.dot(low, dpre, preferred_element_type=F32)
        sent_ref[:R, b * half:(b + 1) * half] = grad[:R, :half].astype(BF16)
        sent_ref[R:, b * half:(b + 1) * half] = grad[R:, half:].astype(BF16)
        dlow = lax.dot_general(out_map, dpre, (((1,), (1,)), ((), ())), preferred_element_type=F32)
        at = blocks * half + b * BLOCK_ROWS
        sent_ref[:, at:at + BLOCK_ROWS] = dlow.astype(BF16)


def project(where, rows, weights, low, out_map, cotan):
    parts, blocks, _, depth = rows.shape
    n_rows, half = cotan.shape
    any_spec = pl.BlockSpec(memory_space=pl.ANY)
    vmem_spec = pl.BlockSpec(memory_space=pltpu.VMEM)
    return pl.pallas_call(
        block_kernel,
        in_specs=[pl.BlockSpec(memory_space=pltpu.SMEM)] + [any_spec] * (1 + parts) + [vmem_spec] * 3,
        out_specs=[vmem_spec, vmem_spec],
        out_shape=[
            jax.ShapeDtypeStruct((n_rows, half), BF16),
            jax.ShapeDtypeStruct((RANKS, blocks * (half + BLOCK_ROWS)), BF16),
        ],
        scratch_shapes=[
            pltpu.VMEM(rows.shape, BF16),
            pltpu.VMEM((parts,) + weights[0].shape, BF16),
            pltpu.VMEM((n_rows, 2 * half), F32),
            pltpu.SemaphoreType.DMA((parts,)),
            pltpu.SemaphoreType.DMA((parts,)),
        ],
        compiler_params=pltpu.CompilerParams(vmem_limit_bytes=VMEM_LIMIT),
        cost_estimate=pl.CostEstimate(
            flops=4 * parts * n_rows * depth * half,
            bytes_accessed=2 * parts * depth * (n_rows + 2 * half),
            transcendentals=n_rows * half),
    )(where, rows, *weights, low, out_map, cotan)


def slot_kernel(slot_ref, shared_ref, out_ref):
    blocks, _ = slot_ref.shape
    width = shared_ref.shape[1] // blocks
    n_out = OWN * Y * N_DP
    row = lax.broadcasted_iota(jnp.int32, (n_out, N_DP), 0)
    lane = lax.broadcasted_iota(jnp.int32, (n_out, N_DP), 1)
    slot = (row & (N_DP - 1)) * OWN + lax.shift_right_logical(row, 7)
    same = (lax.shift_right_logical(row, 5) & (Y - 1)) == (lane & (Y - 1))
    total = None
    for b in range(blocks):
        pick = jnp.where(same & (slot == slot_ref[b:b + 1, :]), 1.0, 0.0).astype(BF16)
        term = jnp.dot(pick, shared_ref[:, b * width:(b + 1) * width], preferred_element_type=F32)
        total = term if total is None else total + term
    for i in range(OWN * Y):
        out_ref[:, i * width:(i + 1) * width] = total[i * N_DP:(i + 1) * N_DP].astype(BF16)


def in_grad_kernel(mine_ref, dlow_ref, rows_ref, out_ref, buf, acc_ref, sems):
    parts, blocks, _, _ = rows_ref.shape

    def load(b):
        return pltpu.make_async_copy(rows_ref.at[:, b], buf.at[b], sems.at[b])

    def used(b):
        return mine_ref[b] + mine_ref[blocks + b] > 0

    for b in range(blocks):
        @pl.when(used(b))
        def _():
            load(b).start()

    acc_ref[...] = jnp.zeros_like(acc_ref)
    for b in range(blocks):
        @pl.when(used(b))
        def _():
            dlow = dlow_ref[:, b * BLOCK_ROWS:(b + 1) * BLOCK_ROWS].astype(F32)
            left = jnp.concatenate(
                [jnp.where(mine_ref[s * blocks + b] > 0, dlow, 0.0) for s in range(OWN)], 0).astype(BF16)
            load(b).wait()

            @pl.loop(0, parts)
            def _(k):
                feature = lax.rem(k - mine_ref[OWN * blocks] + parts, parts)
                acc_ref[feature] += jnp.dot(left, buf[b, k], preferred_element_type=F32)

    out_ref[...] = acc_ref[...].astype(BF16)


def in_grad(mine, dlow, rows):
    parts, blocks, _, depth = rows.shape
    n_out = OWN * RANKS
    vmem_spec = pl.BlockSpec(memory_space=pltpu.VMEM)
    return pl.pallas_call(
        in_grad_kernel,
        in_specs=[pl.BlockSpec(memory_space=pltpu.SMEM), vmem_spec, pl.BlockSpec(memory_space=pl.ANY)],
        out_specs=vmem_spec,
        out_shape=jax.ShapeDtypeStruct((parts, n_out, depth), BF16),
        scratch_shapes=[
            pltpu.VMEM((blocks, parts, BLOCK_ROWS, depth), BF16),
            pltpu.VMEM((parts, n_out, depth), F32),
            pltpu.SemaphoreType.DMA((blocks,)),
        ],
        compiler_params=pltpu.CompilerParams(vmem_limit_bytes=VMEM_LIMIT),
        cost_estimate=pl.CostEstimate(
            flops=2 * parts * n_out * blocks * BLOCK_ROWS * depth,
            bytes_accessed=2 * parts * depth * blocks * BLOCK_ROWS, transcendentals=0),
    )(mine, dlow, rows)


def out_grad_kernel(got_ref, out_ref):
    width = out_ref.shape[2]
    for s in range(OWN):
        out_ref[s] = got_ref[:, s * width:(s + 1) * width].astype(F32)


def body(tokens, gate_up, adapter_in, adapter_out, d_hidden, block_adapter, block_live, owner_slot):
    dp, tensor = lax.axis_index(DP), lax.axis_index(TENSOR)
    d_part, hidden_part = tokens.shape[1], gate_up.shape[2]
    blocks = d_hidden.shape[0] // BLOCK_ROWS
    lanes = RANKS * blocks
    per = RANKS // N_TENSOR

    join = lax.optimization_barrier

    swapped = lax.ppermute(tokens, DP + TENSOR, swap(1))
    in_map = lax.dynamic_index_in_dim(adapter_in, block_adapter[dp], 0, False).reshape(RANKS, d_part)
    low_part = lax.dot_general(in_map, tokens, (((1,), (1,)), ((), ())), preferred_element_type=F32)
    low_sum = exchange(low_part.reshape(N_TENSOR, per, BLOCK_ROWS), TENSOR).sum(0).astype(BF16)
    swapped, low_sum, flat = join((swapped, low_sum, gate_up.reshape(d_part, 2 * hidden_part)))
    rows = lax.all_gather(swapped, DP, axis=0, tiled=False).reshape(Z, Y, BLOCK_ROWS, d_part)

    left, right = hop(flat, "x", X, 1), hop(flat, "x", X, -1)
    own = hop(flat, "c", C, 1)
    low = spread(lax.ppermute(low_sum, DP + TENSOR, swap(0)), DP, N_DP)
    left, right, own, low = join((left, right, own, low))
    far = last_hop(left, right, "x", X)
    weights = [flat, own, left, hop(left, "c", C, 1), right, hop(right, "c", C, 1), far, hop(far, "c", C, 1)]
    low = low.reshape(Z, Y, per, BLOCK_ROWS).transpose(1, 0, 2, 3).reshape(lanes, BLOCK_ROWS)

    local_ids = lax.dynamic_slice_in_dim(block_adapter, tensor * blocks, blocks, 0)
    local_live = lax.dynamic_slice_in_dim(block_live, tensor * blocks, blocks, 0)
    picked = adapter_out[local_ids]
    out_map = jnp.concatenate([
        jnp.pad(picked[:, 0], ((0, 0), (0, 0), (0, hidden_part))),
        jnp.pad(picked[:, 1], ((0, 0), (0, 0), (hidden_part, 0)))], 1)
    where = jnp.concatenate([tensor.astype(jnp.int32)[None], local_live])
    slot_of = owner_slot[block_adapter]
    local_slot = lax.dynamic_slice_in_dim(slot_of, tensor * blocks, blocks, 0)
    mine = jnp.arange(OWN, dtype=jnp.int32)[:, None] + OWN * dp == local_slot[None, :]
    slot_lane = jnp.repeat(slot_of.reshape(N_TENSOR, blocks).T, Y, axis=1)

    hidden, sent = project(where, rows, weights, low, out_map, d_hidden)

    first = exchange(sent, DP)
    split = blocks * hidden_part
    dlow = spread(first[:, split:].astype(F32).sum(0).astype(BF16), DP, N_DP)
    shared = exchange(first[:, :split], TENSOR)
    merged = pl.pallas_call(
        slot_kernel,
        out_shape=jax.ShapeDtypeStruct((N_DP, OWN * Y * hidden_part), BF16),
    )(slot_lane, shared)
    got = exchange(merged, DP)
    in_part = in_grad(jnp.append(mine.reshape(-1).astype(jnp.int32), tensor.astype(jnp.int32)), dlow, rows)
    grad_in = exchange(in_part, TENSOR).astype(F32).sum(0).reshape(OWN, 2, R, d_part)
    grad_out = pl.pallas_call(
        out_grad_kernel,
        out_shape=jax.ShapeDtypeStruct((OWN, RANKS, Y * hidden_part), F32),
    )(got).reshape(OWN, 2, R, Y * hidden_part)
    return hidden, grad_in, grad_out


def solution(mesh):
    mesh = Mesh(mesh.devices.reshape(Z, Y, X, C), DP + TENSOR)

    return jax.shard_map(
        body,
        mesh=mesh,
        in_specs=(P(DP, TENSOR), P(TENSOR, None, DP), P(None, None, None, TENSOR), P(None, None, None, DP),
                  P(TENSOR, DP), P(), P(), P()),
        out_specs=(P(TENSOR, DP), P(DP, None, None, TENSOR), P(DP, None, None, TENSOR)),
        check_vma=False,
    )
```

```python
import jax
import jax.numpy as jnp
from jax import lax
from jax.experimental import pallas as pl
from jax.experimental.pallas import tpu as pltpu
from jax.sharding import Mesh, PartitionSpec as P

R = 16
RANKS = 2 * R
BLOCK_ROWS = 128
Z, Y, X, C = 8, 4, 4, 2
N_DP, N_TENSOR = Z * Y, X * C
OWN = 2
SLOTS = OWN * N_DP
DP, TENSOR = ("z", "y"), ("x", "c")
BF16, F32 = jnp.bfloat16, jnp.float32
VMEM_LIMIT = 48 * 2 ** 20


def swap(skew):
    return [((z * Y + y) * N_TENSOR + t, (((t + skew * z) % Z) * Y + y) * N_TENSOR + z)
            for z in range(Z) for y in range(Y) for t in range(N_TENSOR)]


def exchange(x, axes):
    return lax.all_to_all(x, axes, 0, 0, tiled=True)


def spread(x, axis, n):
    return exchange(jnp.broadcast_to(x[None], (n,) + x.shape), axis)


def hop(x, axis, n, step):
    return lax.ppermute(x, axis, [(i, (i + step) % n) for i in range(n)])


def last_hop(up, down, axis, n):
    pairs = []
    for i in range(n):
        for c in range(C):
            pairs.append((i * C + c, ((i + (1 if c == 0 else -1)) % n) * C + c))
    return lax.ppermute(jnp.where(lax.axis_index("c") == 0, up, down), (axis, "c"), pairs)


def block_kernel(where_ref, rows_ref, *refs):
    weights, refs = refs[:N_TENSOR], refs[N_TENSOR:]
    low_ref, out_map_ref, cot_ref, hidden_ref, sent_ref, x_buf, w_buf, acc_ref, x_sem, w_sem = refs
    parts, blocks, _, depth = x_buf.shape
    t = where_ref[0]

    def place(i):
        x, c = lax.div(t, C), lax.rem(t, C)
        step, other = lax.div(i, C), lax.rem(i, C)
        back = jnp.where(step < 2, step, 5 - step)
        feature = lax.rem(x - back + X, X) * C + lax.rem(c + other, C)
        return lax.rem(feature + t, parts)

    def load(i):
        return pltpu.make_async_copy(rows_ref.at[place(i)], x_buf.at[i], x_sem.at[i])

    for i, weight in enumerate(weights):
        load(i).start()
        pltpu.make_async_copy(weight, w_buf.at[i], w_sem.at[i]).start()
    acc_ref[...] = jnp.zeros_like(acc_ref)

    @pl.loop(0, parts, unroll=True)
    def _(i):
        load(i).wait()
        pltpu.make_async_copy(w_buf.at[i], w_buf.at[i], w_sem.at[i]).wait()
        rows = x_buf[i].reshape(blocks * BLOCK_ROWS, depth)
        acc_ref[...] += jnp.dot(rows, w_buf[i], preferred_element_type=F32)

    half = cot_ref.shape[1]
    for b in range(blocks):
        rows = slice(b * BLOCK_ROWS, (b + 1) * BLOCK_ROWS)
        ranks = slice(b * RANKS, (b + 1) * RANKS)
        low = low_ref[ranks, :]
        out_map = out_map_ref[b]
        pre = acc_ref[rows, :] + lax.dot_general(
            low, out_map, (((0,), (0,)), ((), ())), preferred_element_type=F32)
        gate, up = pre[:, :half], pre[:, half:]
        sigma = jax.nn.sigmoid(gate)
        gated = gate * sigma
        hidden_ref[rows, :] = (gated * up).astype(BF16)
        live = lax.broadcasted_iota(jnp.int32, (BLOCK_ROWS, half), 0) < where_ref[1 + b]
        cotan = jnp.where(live, cot_ref[rows, :].astype(F32), 0.0)
        dgate = cotan * up * sigma * (1.0 + gate * (1.0 - sigma))
        dup = cotan * gated
        dpre = jnp.concatenate([dgate, dup], 1).astype(BF16)
        grad = jnp.dot(low, dpre, preferred_element_type=F32)
        sent_ref[:R, b * half:(b + 1) * half] = grad[:R, :half].astype(BF16)
        sent_ref[R:, b * half:(b + 1) * half] = grad[R:, half:].astype(BF16)
        dlow = lax.dot_general(out_map, dpre, (((1,), (1,)), ((), ())), preferred_element_type=F32)
        at = blocks * half + b * BLOCK_ROWS
        sent_ref[:, at:at + BLOCK_ROWS] = dlow.astype(BF16)


def project(where, rows, weights, low, out_map, cotan):
    parts, blocks, _, depth = rows.shape
    n_rows, half = cotan.shape
    any_spec = pl.BlockSpec(memory_space=pl.ANY)
    vmem_spec = pl.BlockSpec(memory_space=pltpu.VMEM)
    return pl.pallas_call(
        block_kernel,
        in_specs=[pl.BlockSpec(memory_space=pltpu.SMEM)] + [any_spec] * (1 + parts) + [vmem_spec] * 3,
        out_specs=[vmem_spec, vmem_spec],
        out_shape=[
            jax.ShapeDtypeStruct((n_rows, half), BF16),
            jax.ShapeDtypeStruct((RANKS, blocks * (half + BLOCK_ROWS)), BF16),
        ],
        scratch_shapes=[
            pltpu.VMEM(rows.shape, BF16),
            pltpu.VMEM((parts,) + weights[0].shape, BF16),
            pltpu.VMEM((n_rows, 2 * half), F32),
            pltpu.SemaphoreType.DMA((parts,)),
            pltpu.SemaphoreType.DMA((parts,)),
        ],
        compiler_params=pltpu.CompilerParams(vmem_limit_bytes=VMEM_LIMIT),
        cost_estimate=pl.CostEstimate(
            flops=4 * parts * n_rows * depth * half,
            bytes_accessed=2 * parts * depth * (n_rows + 2 * half),
            transcendentals=n_rows * half),
    )(where, rows, *weights, low, out_map, cotan)


def slot_kernel(slot_ref, shared_ref, first_ref, out_ref):
    blocks, _ = slot_ref.shape
    width = shared_ref.shape[1] // blocks - BLOCK_ROWS
    n_out = OWN * Y * N_DP
    row = lax.broadcasted_iota(jnp.int32, (n_out, N_DP), 0)
    lane = lax.broadcasted_iota(jnp.int32, (n_out, N_DP), 1)
    slot = (row & (N_DP - 1)) * OWN + lax.shift_right_logical(row, 7)
    same = (lax.shift_right_logical(row, 5) & (Y - 1)) == (lane & (Y - 1))
    total = None
    for b in range(blocks):
        pick = jnp.where(same & (slot == slot_ref[b:b + 1, :]), 1.0, 0.0).astype(BF16)
        term = jnp.dot(pick, shared_ref[:, b * width:(b + 1) * width], preferred_element_type=F32)
        total = term if total is None else total + term
    for i in range(OWN * Y):
        out_ref[:, i * width:(i + 1) * width] = total[i * N_DP:(i + 1) * N_DP].astype(BF16)
    dlow = jnp.sum(first_ref[:, blocks * width:].astype(F32), axis=0, keepdims=True)
    out_ref[:, OWN * Y * width:] = jnp.broadcast_to(dlow, (N_DP, dlow.shape[1])).astype(BF16)


def in_grad_kernel(mine_ref, got_ref, rows_ref, out_ref, buf, acc_ref, sems):
    parts, blocks, _, _ = rows_ref.shape
    start = got_ref.shape[1] - blocks * BLOCK_ROWS

    def load(b):
        return pltpu.make_async_copy(rows_ref.at[:, b], buf.at[b], sems.at[b])

    def used(b):
        return mine_ref[b] + mine_ref[blocks + b] > 0

    for b in range(blocks):
        @pl.when(used(b))
        def _():
            load(b).start()

    acc_ref[...] = jnp.zeros_like(acc_ref)
    for b in range(blocks):
        @pl.when(used(b))
        def _():
            dlow = got_ref[:, start + b * BLOCK_ROWS:start + (b + 1) * BLOCK_ROWS].astype(F32)
            left = jnp.concatenate(
                [jnp.where(mine_ref[s * blocks + b] > 0, dlow, 0.0) for s in range(OWN)], 0).astype(BF16)
            load(b).wait()

            @pl.loop(0, parts)
            def _(k):
                feature = lax.rem(k - mine_ref[OWN * blocks] + parts, parts)
                acc_ref[feature] += jnp.dot(left, buf[b, k], preferred_element_type=F32)

    out_ref[...] = acc_ref[...].astype(BF16)


def in_grad(mine, got, rows):
    parts, blocks, _, depth = rows.shape
    n_out = OWN * RANKS
    vmem_spec = pl.BlockSpec(memory_space=pltpu.VMEM)
    return pl.pallas_call(
        in_grad_kernel,
        in_specs=[pl.BlockSpec(memory_space=pltpu.SMEM), vmem_spec, pl.BlockSpec(memory_space=pl.ANY)],
        out_specs=vmem_spec,
        out_shape=jax.ShapeDtypeStruct((parts, n_out, depth), BF16),
        scratch_shapes=[
            pltpu.VMEM((blocks, parts, BLOCK_ROWS, depth), BF16),
            pltpu.VMEM((parts, n_out, depth), F32),
            pltpu.SemaphoreType.DMA((blocks,)),
        ],
        compiler_params=pltpu.CompilerParams(vmem_limit_bytes=VMEM_LIMIT),
        cost_estimate=pl.CostEstimate(
            flops=2 * parts * n_out * blocks * BLOCK_ROWS * depth,
            bytes_accessed=2 * parts * depth * blocks * BLOCK_ROWS, transcendentals=0),
    )(mine, got, rows)


def out_grad_kernel(got_ref, out_ref):
    width = out_ref.shape[2]
    for s in range(OWN):
        out_ref[s] = got_ref[:, s * width:(s + 1) * width].astype(F32)


def body(tokens, gate_up, adapter_in, adapter_out, d_hidden, block_adapter, block_live, owner_slot):
    dp, tensor = lax.axis_index(DP), lax.axis_index(TENSOR)
    d_part, hidden_part = tokens.shape[1], gate_up.shape[2]
    blocks = d_hidden.shape[0] // BLOCK_ROWS
    lanes = RANKS * blocks
    per = RANKS // N_TENSOR

    join = lax.optimization_barrier

    swapped = lax.ppermute(tokens, DP + TENSOR, swap(1))
    in_map = lax.dynamic_index_in_dim(adapter_in, block_adapter[dp], 0, False).reshape(RANKS, d_part)
    low_part = lax.dot_general(in_map, tokens, (((1,), (1,)), ((), ())), preferred_element_type=F32)
    low_sum = exchange(low_part.reshape(N_TENSOR, per, BLOCK_ROWS), TENSOR).sum(0).astype(BF16)
    swapped, low_sum, gate_up = join((swapped, low_sum, gate_up))
    rows = lax.all_gather(swapped, DP, axis=0, tiled=False).reshape(Z, Y, BLOCK_ROWS, d_part)

    flat = gate_up.reshape(d_part, 2 * hidden_part)
    left, right = hop(flat, "x", X, 1), hop(flat, "x", X, -1)
    own = hop(flat, "c", C, 1)
    low = spread(lax.ppermute(low_sum, DP + TENSOR, swap(0)), DP, N_DP)
    left, right, own, low = join((left, right, own, low))
    far = last_hop(left, right, "x", X)
    weights = [flat, own, left, hop(left, "c", C, 1), right, hop(right, "c", C, 1), far, hop(far, "c", C, 1)]
    low = low.reshape(Z, Y, per, BLOCK_ROWS).transpose(1, 0, 2, 3).reshape(lanes, BLOCK_ROWS)

    local_ids = lax.dynamic_slice_in_dim(block_adapter, tensor * blocks, blocks, 0)
    local_live = lax.dynamic_slice_in_dim(block_live, tensor * blocks, blocks, 0)
    picked = adapter_out[local_ids]
    out_map = jnp.concatenate([
        jnp.pad(picked[:, 0], ((0, 0), (0, 0), (0, hidden_part))),
        jnp.pad(picked[:, 1], ((0, 0), (0, 0), (hidden_part, 0)))], 1)
    where = jnp.concatenate([tensor.astype(jnp.int32)[None], local_live])
    slot_of = owner_slot[block_adapter]
    local_slot = lax.dynamic_slice_in_dim(slot_of, tensor * blocks, blocks, 0)
    mine = jnp.arange(OWN, dtype=jnp.int32)[:, None] + OWN * dp == local_slot[None, :]
    slot_lane = jnp.repeat(slot_of.reshape(N_TENSOR, blocks).T, Y, axis=1)

    hidden, sent = project(where, rows, weights, low, out_map, d_hidden)

    first = exchange(sent, DP)
    shared = exchange(first, TENSOR)
    merged = pl.pallas_call(
        slot_kernel,
        out_shape=jax.ShapeDtypeStruct((N_DP, OWN * Y * hidden_part + blocks * BLOCK_ROWS), BF16),
    )(slot_lane, shared, first)
    got = exchange(merged, DP)
    in_part = in_grad(jnp.append(mine.reshape(-1).astype(jnp.int32), tensor.astype(jnp.int32)), got, rows)
    grad_in = exchange(in_part, TENSOR).astype(F32).sum(0).reshape(OWN, 2, R, d_part)
    grad_out = pl.pallas_call(
        out_grad_kernel,
        out_shape=jax.ShapeDtypeStruct((OWN, RANKS, Y * hidden_part), F32),
    )(got).reshape(OWN, 2, R, Y * hidden_part)
    return hidden, grad_in, grad_out


def solution(mesh):
    mesh = Mesh(mesh.devices.reshape(Z, Y, X, C), DP + TENSOR)

    return jax.shard_map(
        body,
        mesh=mesh,
        in_specs=(P(DP, TENSOR), P(TENSOR, None, DP), P(None, None, None, TENSOR), P(None, None, None, DP),
                  P(TENSOR, DP), P(), P(), P()),
        out_specs=(P(TENSOR, DP), P(DP, None, None, TENSOR), P(DP, None, None, TENSOR)),
        check_vma=False,
    )
```

```python
import jax
import jax.numpy as jnp
from jax import lax
from jax.experimental import pallas as pl
from jax.experimental.pallas import tpu as pltpu
from jax.sharding import Mesh, PartitionSpec as P

R = 16
RANKS = 2 * R
BLOCK_ROWS = 128
Z, Y, X, C = 8, 4, 4, 2
N_DP, N_TENSOR = Z * Y, X * C
OWN = 2
SLOTS = OWN * N_DP
DP, TENSOR = ("z", "y"), ("x", "c")
BF16, F32 = jnp.bfloat16, jnp.float32
VMEM_LIMIT = 48 * 2 ** 20


STEPS = (1, -1, 2, -2, 3, -3, 0, 4)


def swap(place):
    return [((z * Y + y) * N_TENSOR + t, (place(z, t) * Y + y) * N_TENSOR + z)
            for z in range(Z) for y in range(Y) for t in range(N_TENSOR)]


def exchange(x, axes):
    return lax.all_to_all(x, axes, 0, 0, tiled=True)


def spread(x, axis, n):
    return exchange(jnp.broadcast_to(x[None], (n,) + x.shape), axis)


def hop(x, axis, n, step):
    return lax.ppermute(x, axis, [(i, (i + step) % n) for i in range(n)])


def last_hop(up, down, axis, n):
    pairs = []
    for i in range(n):
        for c in range(C):
            pairs.append((i * C + c, ((i + (1 if c == 0 else -1)) % n) * C + c))
    return lax.ppermute(jnp.where(lax.axis_index("c") == 0, up, down), (axis, "c"), pairs)


def block_kernel(where_ref, rows_ref, *refs):
    weights, refs = refs[:N_TENSOR], refs[N_TENSOR:]
    low_ref, out_map_ref, cot_ref, hidden_ref, sent_ref, x_buf, w_buf, acc_ref, x_sem, w_sem = refs
    parts, blocks, _, depth = x_buf.shape
    t = where_ref[0]

    def place(i):
        x, c = lax.rem(lax.div(t, C) - (0, 1, 3, 2)[i // C] + X, X), lax.rem(t + i % C, C)
        step = jnp.where(c == 0, x + 1, -x - 1)
        step = jnp.where(x == X - 1, jnp.where(c == 0, 0, 4), step)
        return lax.rem(t + step + parts, parts)

    def load(i):
        return pltpu.make_async_copy(rows_ref.at[:, place(i)], x_buf.at[i], x_sem.at[i])

    for i, weight in enumerate(weights):
        load(i).start()
        pltpu.make_async_copy(weight, w_buf.at[i], w_sem.at[i]).start()

    for i, weight in enumerate(weights):
        load(i).wait()
        pltpu.make_async_copy(weight, w_buf.at[i], w_sem.at[i]).wait()
        rows = x_buf[i].reshape(blocks * BLOCK_ROWS, depth)
        part = jnp.dot(rows, w_buf[i], preferred_element_type=F32)
        acc_ref[...] = part if i == 0 else acc_ref[...] + part

    half = cot_ref.shape[1]
    for b in range(blocks):
        rows = slice(b * BLOCK_ROWS, (b + 1) * BLOCK_ROWS)
        ranks = slice(b * RANKS, (b + 1) * RANKS)
        low = low_ref[ranks, :]
        out_map = out_map_ref[b]
        pre = acc_ref[rows, :] + lax.dot_general(
            low, out_map, (((0,), (0,)), ((), ())), preferred_element_type=F32)
        gate, up = pre[:, :half], pre[:, half:]
        sigma = jax.nn.sigmoid(gate)
        gated = gate * sigma
        hidden_ref[rows, :] = (gated * up).astype(BF16)
        live = lax.broadcasted_iota(jnp.int32, (BLOCK_ROWS, half), 0) < where_ref[1 + b]
        cotan = jnp.where(live, cot_ref[rows, :].astype(F32), 0.0)
        dgate = cotan * up * sigma * (1.0 + gate * (1.0 - sigma))
        dup = cotan * gated
        dpre = jnp.concatenate([dgate, dup], 1).astype(BF16)
        grad = jnp.dot(low, dpre, preferred_element_type=F32)
        sent_ref[:R, b * half:(b + 1) * half] = grad[:R, :half].astype(BF16)
        sent_ref[R:, b * half:(b + 1) * half] = grad[R:, half:].astype(BF16)
        dlow = lax.dot_general(out_map, dpre, (((1,), (1,)), ((), ())), preferred_element_type=F32)
        at = blocks * half + b * BLOCK_ROWS
        sent_ref[:, at:at + BLOCK_ROWS] = dlow.astype(BF16)


def project(where, rows, weights, low, out_map, cotan):
    blocks, parts, _, depth = rows.shape
    n_rows, half = cotan.shape
    any_spec = pl.BlockSpec(memory_space=pl.ANY)
    vmem_spec = pl.BlockSpec(memory_space=pltpu.VMEM)
    return pl.pallas_call(
        block_kernel,
        in_specs=[pl.BlockSpec(memory_space=pltpu.SMEM)] + [any_spec] * (1 + parts) + [vmem_spec] * 3,
        out_specs=[vmem_spec, vmem_spec],
        out_shape=[
            jax.ShapeDtypeStruct((n_rows, half), BF16),
            jax.ShapeDtypeStruct((RANKS, blocks * (half + BLOCK_ROWS)), BF16),
        ],
        scratch_shapes=[
            pltpu.VMEM((parts, blocks, BLOCK_ROWS, depth), BF16),
            pltpu.VMEM((parts,) + weights[0].shape, BF16),
            pltpu.VMEM((n_rows, 2 * half), F32),
            pltpu.SemaphoreType.DMA((parts,)),
            pltpu.SemaphoreType.DMA((parts,)),
        ],
        compiler_params=pltpu.CompilerParams(vmem_limit_bytes=VMEM_LIMIT),
        cost_estimate=pl.CostEstimate(
            flops=4 * parts * n_rows * depth * half,
            bytes_accessed=2 * parts * depth * (n_rows + 2 * half),
            transcendentals=n_rows * half),
    )(where, rows, *weights, low, out_map, cotan)


def slot_kernel(slot_ref, shared_ref, first_ref, out_ref):
    blocks, _ = slot_ref.shape
    width = shared_ref.shape[1] // blocks - BLOCK_ROWS
    n_out = OWN * Y * N_DP
    row = lax.broadcasted_iota(jnp.int32, (n_out, N_DP), 0)
    lane = lax.broadcasted_iota(jnp.int32, (n_out, N_DP), 1)
    slot = (row & (N_DP - 1)) * OWN + lax.shift_right_logical(row, 7)
    same = (lax.shift_right_logical(row, 5) & (Y - 1)) == (lane & (Y - 1))
    total = None
    for b in range(blocks):
        pick = jnp.where(same & (slot == slot_ref[b:b + 1, :]), 1.0, 0.0).astype(BF16)
        term = jnp.dot(pick, shared_ref[:, b * width:(b + 1) * width], preferred_element_type=F32)
        total = term if total is None else total + term
    for i in range(OWN * Y):
        out_ref[:, i * width:(i + 1) * width] = total[i * N_DP:(i + 1) * N_DP].astype(BF16)
    dlow = jnp.sum(first_ref[:, blocks * width:].astype(F32), axis=0, keepdims=True)
    out_ref[:, OWN * Y * width:] = jnp.broadcast_to(dlow, (N_DP, dlow.shape[1])).astype(BF16)


def in_grad_kernel(mine_ref, got_ref, rows_ref, out_ref, buf, acc_ref, sems):
    blocks, parts, _, _ = rows_ref.shape
    start = got_ref.shape[1] - blocks * BLOCK_ROWS

    def load(b):
        return pltpu.make_async_copy(rows_ref.at[b], buf.at[b], sems.at[b])

    def used(b):
        return mine_ref[b] + mine_ref[blocks + b] > 0

    for b in range(blocks):
        @pl.when(used(b))
        def _():
            load(b).start()

    acc_ref[...] = jnp.zeros_like(acc_ref)
    for b in range(blocks):
        @pl.when(used(b))
        def _():
            dlow = got_ref[:, start + b * BLOCK_ROWS:start + (b + 1) * BLOCK_ROWS].astype(F32)
            left = jnp.concatenate(
                [jnp.where(mine_ref[s * blocks + b] > 0, dlow, 0.0) for s in range(OWN)], 0).astype(BF16)
            load(b).wait()

            for feature, step in enumerate(STEPS):
                place = lax.rem(mine_ref[OWN * blocks] + step + parts, parts)
                acc_ref[feature] += jnp.dot(left, buf[b, place], preferred_element_type=F32)

    out_ref[...] = acc_ref[...].astype(BF16)


def in_grad(mine, got, rows):
    blocks, parts, _, depth = rows.shape
    n_out = OWN * RANKS
    vmem_spec = pl.BlockSpec(memory_space=pltpu.VMEM)
    return pl.pallas_call(
        in_grad_kernel,
        in_specs=[pl.BlockSpec(memory_space=pltpu.SMEM), vmem_spec, pl.BlockSpec(memory_space=pl.ANY)],
        out_specs=vmem_spec,
        out_shape=jax.ShapeDtypeStruct((parts, n_out, depth), BF16),
        scratch_shapes=[
            pltpu.VMEM((blocks, parts, BLOCK_ROWS, depth), BF16),
            pltpu.VMEM((parts, n_out, depth), F32),
            pltpu.SemaphoreType.DMA((blocks,)),
        ],
        compiler_params=pltpu.CompilerParams(vmem_limit_bytes=VMEM_LIMIT),
        cost_estimate=pl.CostEstimate(
            flops=2 * parts * n_out * blocks * BLOCK_ROWS * depth,
            bytes_accessed=2 * parts * depth * blocks * BLOCK_ROWS, transcendentals=0),
    )(mine, got, rows)


def out_grad_kernel(got_ref, out_ref):
    width = out_ref.shape[2]
    for s in range(OWN):
        out_ref[s] = got_ref[:, s * width:(s + 1) * width].astype(F32)


def body(tokens, gate_up, adapter_in, adapter_out, d_hidden, block_adapter, block_live, owner_slot):
    dp, tensor = lax.axis_index(DP), lax.axis_index(TENSOR)
    d_part, hidden_part = tokens.shape[1], gate_up.shape[2]
    blocks = d_hidden.shape[0] // BLOCK_ROWS
    lanes = RANKS * blocks
    per = RANKS // N_TENSOR

    join = lax.optimization_barrier

    swapped = lax.ppermute(tokens, DP + TENSOR, swap(lambda z, t: (z + STEPS[t]) % Z))
    in_map = lax.dynamic_index_in_dim(adapter_in, block_adapter[dp], 0, False).reshape(RANKS, d_part)
    low_part = lax.dot_general(in_map, tokens, (((1,), (1,)), ((), ())), preferred_element_type=F32)
    low_sum = exchange(low_part.reshape(N_TENSOR, per, BLOCK_ROWS), TENSOR).sum(0).astype(BF16)
    rows = lax.all_gather(swapped, ("y", "z"), axis=0, tiled=False).reshape(Y, Z, BLOCK_ROWS, d_part)
    low_sum, gate_up, _ = join((low_sum, gate_up, swapped))

    flat = gate_up.reshape(d_part, 2 * hidden_part)
    left, right = hop(flat, "x", X, 1), hop(flat, "x", X, -1)
    own = hop(flat, "c", C, 1)
    low = spread(lax.ppermute(low_sum, DP + TENSOR, swap(lambda z, t: t)), DP, N_DP)
    left, right, own, low = join((left, right, own, low))
    far = last_hop(left, right, "x", X)
    weights = [flat, own, left, hop(left, "c", C, 1), right, hop(right, "c", C, 1), far, hop(far, "c", C, 1)]
    low = low.reshape(Z, Y, per, BLOCK_ROWS).transpose(1, 0, 2, 3).reshape(lanes, BLOCK_ROWS)

    local_ids = lax.dynamic_slice_in_dim(block_adapter, tensor * blocks, blocks, 0)
    local_live = lax.dynamic_slice_in_dim(block_live, tensor * blocks, blocks, 0)
    picked = adapter_out[local_ids]
    out_map = jnp.concatenate([
        jnp.pad(picked[:, 0], ((0, 0), (0, 0), (0, hidden_part))),
        jnp.pad(picked[:, 1], ((0, 0), (0, 0), (hidden_part, 0)))], 1)
    where = jnp.concatenate([tensor.astype(jnp.int32)[None], local_live])
    slot_of = owner_slot[block_adapter]
    local_slot = lax.dynamic_slice_in_dim(slot_of, tensor * blocks, blocks, 0)
    mine = jnp.arange(OWN, dtype=jnp.int32)[:, None] + OWN * dp == local_slot[None, :]
    slot_lane = jnp.repeat(slot_of.reshape(N_TENSOR, blocks).T, Y, axis=1)

    hidden, sent = project(where, rows, weights, low, out_map, d_hidden)

    first = exchange(sent, DP)
    shared = exchange(first, TENSOR)
    merged = pl.pallas_call(
        slot_kernel,
        out_shape=jax.ShapeDtypeStruct((N_DP, OWN * Y * hidden_part + blocks * BLOCK_ROWS), BF16),
    )(slot_lane, shared, first)
    got = exchange(merged, DP)
    in_part = in_grad(jnp.append(mine.reshape(-1).astype(jnp.int32), tensor.astype(jnp.int32)), got, rows)
    grad_in = exchange(in_part, TENSOR).astype(F32).sum(0).reshape(OWN, 2, R, d_part)
    grad_out = pl.pallas_call(
        out_grad_kernel,
        out_shape=jax.ShapeDtypeStruct((OWN, RANKS, Y * hidden_part), F32),
    )(got).reshape(OWN, 2, R, Y * hidden_part)
    return hidden, grad_in, grad_out


def solution(mesh):
    mesh = Mesh(mesh.devices.reshape(Z, Y, X, C), DP + TENSOR)

    return jax.shard_map(
        body,
        mesh=mesh,
        in_specs=(P(DP, TENSOR), P(TENSOR, None, DP), P(None, None, None, TENSOR), P(None, None, None, DP),
                  P(TENSOR, DP), P(), P(), P()),
        out_specs=(P(TENSOR, DP), P(DP, None, None, TENSOR), P(DP, None, None, TENSOR)),
        check_vma=False,
    )
```

```python
import jax
import jax.numpy as jnp
from jax import lax
from jax.experimental import pallas as pl
from jax.experimental.pallas import tpu as pltpu
from jax.sharding import Mesh, PartitionSpec as P

R = 16
RANKS = 2 * R
BLOCK_ROWS = 128
Z, Y, X, C = 8, 4, 4, 2
N_DP, N_TENSOR = Z * Y, X * C
OWN = 2
SLOTS = OWN * N_DP
DP, TENSOR = ("z", "y"), ("x", "c")
BF16, F32 = jnp.bfloat16, jnp.float32
VMEM_LIMIT = 48 * 2 ** 20


STEPS = (1, -1, 2, -2, 3, -3, 0, 4)


def swap(place):
    return [((z * Y + y) * N_TENSOR + t, (place(z, t) * Y + y) * N_TENSOR + z)
            for z in range(Z) for y in range(Y) for t in range(N_TENSOR)]


def exchange(x, axes):
    return lax.all_to_all(x, axes, 0, 0, tiled=True)


def spread(x, axis, n):
    return exchange(jnp.broadcast_to(x[None], (n,) + x.shape), axis)


def hop(x, axis, n, step):
    return lax.ppermute(x, axis, [(i, (i + step) % n) for i in range(n)])


def last_hop(up, down, axis, n):
    pairs = []
    for i in range(n):
        for c in range(C):
            pairs.append((i * C + c, ((i + (1 if c == 0 else -1)) % n) * C + c))
    return lax.ppermute(jnp.where(lax.axis_index("c") == 0, up, down), (axis, "c"), pairs)


def block_kernel(where_ref, rows_ref, *refs):
    weights, refs = refs[:N_TENSOR], refs[N_TENSOR:]
    low_ref, out_map_ref, cot_ref, hidden_ref, sent_ref, x_buf, w_buf, acc_ref, x_sem, w_sem = refs
    parts, blocks, _, depth = x_buf.shape
    t = where_ref[0]

    def place(i):
        x, c = lax.rem(lax.div(t, C) - (0, 1, 3, 2)[i // C] + X, X), lax.rem(t + i % C, C)
        step = jnp.where(c == 0, x + 1, -x - 1)
        step = jnp.where(x == X - 1, jnp.where(c == 0, 0, 4), step)
        return lax.rem(t + step + parts, parts)

    def load(i):
        return pltpu.make_async_copy(rows_ref.at[:, place(i)], x_buf.at[i], x_sem.at[i])

    for i, weight in enumerate(weights):
        load(i).start()
        pltpu.make_async_copy(weight, w_buf.at[i], w_sem.at[i]).start()

    for i, weight in enumerate(weights):
        load(i).wait()
        pltpu.make_async_copy(weight, w_buf.at[i], w_sem.at[i]).wait()
        rows = x_buf[i].reshape(blocks * BLOCK_ROWS, depth)
        part = jnp.dot(rows, w_buf[i], preferred_element_type=F32)
        acc_ref[...] = part if i == 0 else acc_ref[...] + part

    half = cot_ref.shape[1]
    for b in range(blocks):
        rows = slice(b * BLOCK_ROWS, (b + 1) * BLOCK_ROWS)
        ranks = slice(b * RANKS, (b + 1) * RANKS)
        low = low_ref[ranks, :]
        out_map = out_map_ref[b]
        pre = acc_ref[rows, :] + lax.dot_general(
            low, out_map, (((0,), (0,)), ((), ())), preferred_element_type=F32)
        gate, up = pre[:, :half], pre[:, half:]
        sigma = jax.nn.sigmoid(gate)
        gated = gate * sigma
        hidden_ref[rows, :] = (gated * up).astype(BF16)
        live = lax.broadcasted_iota(jnp.int32, (BLOCK_ROWS, half), 0) < where_ref[1 + b]
        cotan = jnp.where(live, cot_ref[rows, :].astype(F32), 0.0)
        dgate = cotan * up * sigma * (1.0 + gate * (1.0 - sigma))
        dup = cotan * gated
        dpre = jnp.concatenate([dgate, dup], 1).astype(BF16)
        grad = jnp.dot(low, dpre, preferred_element_type=F32)
        sent_ref[:R, b * half:(b + 1) * half] = grad[:R, :half].astype(BF16)
        sent_ref[R:, b * half:(b + 1) * half] = grad[R:, half:].astype(BF16)
        dlow = lax.dot_general(out_map, dpre, (((1,), (1,)), ((), ())), preferred_element_type=F32)
        at = blocks * half + b * BLOCK_ROWS
        sent_ref[:, at:at + BLOCK_ROWS] = dlow.astype(BF16)


def project(where, rows, weights, low, out_map, cotan):
    blocks, parts, _, depth = rows.shape
    n_rows, half = cotan.shape
    any_spec = pl.BlockSpec(memory_space=pl.ANY)
    vmem_spec = pl.BlockSpec(memory_space=pltpu.VMEM)
    return pl.pallas_call(
        block_kernel,
        in_specs=[pl.BlockSpec(memory_space=pltpu.SMEM)] + [any_spec] * (1 + parts) + [vmem_spec] * 3,
        out_specs=[vmem_spec, vmem_spec],
        out_shape=[
            jax.ShapeDtypeStruct((n_rows, half), BF16),
            jax.ShapeDtypeStruct((RANKS, blocks * (half + BLOCK_ROWS)), BF16),
        ],
        scratch_shapes=[
            pltpu.VMEM((parts, blocks, BLOCK_ROWS, depth), BF16),
            pltpu.VMEM((parts,) + weights[0].shape, BF16),
            pltpu.VMEM((n_rows, 2 * half), F32),
            pltpu.SemaphoreType.DMA((parts,)),
            pltpu.SemaphoreType.DMA((parts,)),
        ],
        compiler_params=pltpu.CompilerParams(vmem_limit_bytes=VMEM_LIMIT),
        cost_estimate=pl.CostEstimate(
            flops=4 * parts * n_rows * depth * half,
            bytes_accessed=2 * parts * depth * (n_rows + 2 * half),
            transcendentals=n_rows * half),
    )(where, rows, *weights, low, out_map, cotan)


def slot_kernel(slot_ref, shared_ref, out_ref):
    blocks, _ = slot_ref.shape
    width = shared_ref.shape[1] // blocks - BLOCK_ROWS
    n_out = OWN * Y * N_DP
    row = lax.broadcasted_iota(jnp.int32, (n_out, N_DP), 0)
    lane = lax.broadcasted_iota(jnp.int32, (n_out, N_DP), 1)
    slot = (row & (N_DP - 1)) * OWN + lax.shift_right_logical(row, 7)
    same = (lax.shift_right_logical(row, 5) & (Y - 1)) == (lane & (Y - 1))
    total = None
    for b in range(blocks):
        pick = jnp.where(same & (slot == slot_ref[b:b + 1, :]), 1.0, 0.0).astype(BF16)
        term = jnp.dot(pick, shared_ref[:, b * width:(b + 1) * width], preferred_element_type=F32)
        total = term if total is None else total + term
    for i in range(OWN * Y):
        out_ref[:, i * width:(i + 1) * width] = total[i * N_DP:(i + 1) * N_DP].astype(BF16)


def in_grad_kernel(mine_ref, dlow_ref, rows_ref, acc_ref, buf, sems):
    blocks, parts, _, _ = rows_ref.shape

    def load(b):
        return pltpu.make_async_copy(rows_ref.at[b], buf.at[b], sems.at[b])

    def used(b):
        return mine_ref[b] + mine_ref[blocks + b] > 0

    for b in range(blocks):
        @pl.when(used(b))
        def _():
            load(b).start()

    acc_ref[...] = jnp.zeros_like(acc_ref)
    for b in range(blocks):
        @pl.when(used(b))
        def _():
            dlow = dlow_ref[:, b * BLOCK_ROWS:(b + 1) * BLOCK_ROWS].astype(F32)
            left = jnp.concatenate(
                [jnp.where(mine_ref[s * blocks + b] > 0, dlow, 0.0) for s in range(OWN)], 0).astype(BF16)
            load(b).wait()

            for feature, step in enumerate(STEPS):
                place = lax.rem(mine_ref[OWN * blocks] + step + parts, parts)
                acc_ref[feature] += jnp.dot(left, buf[b, place], preferred_element_type=F32)


def in_grad(mine, dlow, rows):
    blocks, parts, _, depth = rows.shape
    n_out = OWN * RANKS
    vmem_spec = pl.BlockSpec(memory_space=pltpu.VMEM)
    return pl.pallas_call(
        in_grad_kernel,
        in_specs=[pl.BlockSpec(memory_space=pltpu.SMEM), vmem_spec, pl.BlockSpec(memory_space=pl.ANY)],
        out_specs=vmem_spec,
        out_shape=jax.ShapeDtypeStruct((parts, n_out, depth), F32),
        scratch_shapes=[
            pltpu.VMEM((blocks, parts, BLOCK_ROWS, depth), BF16),
            pltpu.SemaphoreType.DMA((blocks,)),
        ],
        compiler_params=pltpu.CompilerParams(vmem_limit_bytes=VMEM_LIMIT),
        cost_estimate=pl.CostEstimate(
            flops=2 * parts * n_out * blocks * BLOCK_ROWS * depth,
            bytes_accessed=2 * parts * depth * blocks * BLOCK_ROWS, transcendentals=0),
    )(mine, dlow, rows)


def out_grad_kernel(got_ref, out_ref):
    width = out_ref.shape[2]
    for s in range(OWN):
        out_ref[s] = got_ref[:, s * width:(s + 1) * width].astype(F32)


def body(tokens, gate_up, adapter_in, adapter_out, d_hidden, block_adapter, block_live, owner_slot):
    dp, tensor = lax.axis_index(DP), lax.axis_index(TENSOR)
    d_part, hidden_part = tokens.shape[1], gate_up.shape[2]
    blocks = d_hidden.shape[0] // BLOCK_ROWS
    lanes = RANKS * blocks
    per = RANKS // N_TENSOR

    join = lax.optimization_barrier

    swapped = lax.ppermute(tokens, DP + TENSOR, swap(lambda z, t: (z + STEPS[t]) % Z))
    in_map = lax.dynamic_index_in_dim(adapter_in, block_adapter[dp], 0, False).reshape(RANKS, d_part)
    low_part = lax.dot_general(in_map, tokens, (((1,), (1,)), ((), ())), preferred_element_type=F32)
    low_sum = exchange(low_part.reshape(N_TENSOR, per, BLOCK_ROWS), TENSOR).sum(0).astype(BF16)
    rows = lax.all_gather(swapped, ("y", "z"), axis=0, tiled=False).reshape(Y, Z, BLOCK_ROWS, d_part)
    low_sum, gate_up, _ = join((low_sum, gate_up, swapped))

    flat = gate_up.reshape(d_part, 2 * hidden_part)
    left, right = hop(flat, "x", X, 1), hop(flat, "x", X, -1)
    own = hop(flat, "c", C, 1)
    low = spread(lax.ppermute(low_sum, DP + TENSOR, swap(lambda z, t: t)), DP, N_DP)
    left, right, own, low = join((left, right, own, low))
    far = last_hop(left, right, "x", X)
    weights = [flat, own, left, hop(left, "c", C, 1), right, hop(right, "c", C, 1), far, hop(far, "c", C, 1)]
    low = low.reshape(Z, Y, per, BLOCK_ROWS).transpose(1, 0, 2, 3).reshape(lanes, BLOCK_ROWS)

    local_ids = lax.dynamic_slice_in_dim(block_adapter, tensor * blocks, blocks, 0)
    local_live = lax.dynamic_slice_in_dim(block_live, tensor * blocks, blocks, 0)
    picked = adapter_out[local_ids]
    out_map = jnp.concatenate([
        jnp.pad(picked[:, 0], ((0, 0), (0, 0), (0, hidden_part))),
        jnp.pad(picked[:, 1], ((0, 0), (0, 0), (hidden_part, 0)))], 1)
    where = jnp.concatenate([tensor.astype(jnp.int32)[None], local_live])
    slot_of = owner_slot[block_adapter]
    local_slot = lax.dynamic_slice_in_dim(slot_of, tensor * blocks, blocks, 0)
    mine = jnp.arange(OWN, dtype=jnp.int32)[:, None] + OWN * dp == local_slot[None, :]
    slot_lane = jnp.repeat(slot_of.reshape(N_TENSOR, blocks).T, Y, axis=1)

    hidden, sent = project(where, rows, weights, low, out_map, d_hidden)

    first = exchange(sent, DP)
    dlow = spread(first[:, blocks * hidden_part:].astype(F32).sum(0).astype(BF16), DP, N_DP)
    in_part = in_grad(jnp.append(mine.reshape(-1).astype(jnp.int32), tensor.astype(jnp.int32)), dlow, rows)
    in_part, first = join((in_part, first))
    grad_in = lax.psum_scatter(in_part, TENSOR, scatter_dimension=0, tiled=True).reshape(OWN, 2, R, d_part)
    shared = exchange(first, TENSOR)
    merged = pl.pallas_call(
        slot_kernel,
        out_shape=jax.ShapeDtypeStruct((N_DP, OWN * Y * hidden_part), BF16),
    )(slot_lane, shared)
    got = exchange(merged, DP)
    grad_out = pl.pallas_call(
        out_grad_kernel,
        out_shape=jax.ShapeDtypeStruct((OWN, RANKS, Y * hidden_part), F32),
    )(got).reshape(OWN, 2, R, Y * hidden_part)
    return hidden, grad_in, grad_out


def solution(mesh):
    mesh = Mesh(mesh.devices.reshape(Z, Y, X, C), DP + TENSOR)

    return jax.shard_map(
        body,
        mesh=mesh,
        in_specs=(P(DP, TENSOR), P(TENSOR, None, DP), P(None, None, None, TENSOR), P(None, None, None, DP),
                  P(TENSOR, DP), P(), P(), P()),
        out_specs=(P(TENSOR, DP), P(DP, None, None, TENSOR), P(DP, None, None, TENSOR)),
        check_vma=False,
    )
```

```python
import jax
import jax.numpy as jnp
from jax import lax
from jax.experimental import pallas as pl
from jax.experimental.pallas import tpu as pltpu
from jax.sharding import Mesh, PartitionSpec as P

R = 16
RANKS = 2 * R
BLOCK_ROWS = 128
Z, Y, X, C = 8, 4, 4, 2
N_DP, N_TENSOR = Z * Y, X * C
OWN = 2
SLOTS = OWN * N_DP
DP, TENSOR = ("z", "y"), ("x", "c")
BF16, F32 = jnp.bfloat16, jnp.float32
VMEM_LIMIT = 48 * 2 ** 20


STEPS = (1, -1, 2, -2, 3, -3, 0, 4)


def swap(place):
    return [((z * Y + y) * N_TENSOR + t, (place(z, t) * Y + y) * N_TENSOR + z)
            for z in range(Z) for y in range(Y) for t in range(N_TENSOR)]


def exchange(x, axes):
    return lax.all_to_all(x, axes, 0, 0, tiled=True)


def spread(x, axis, n):
    return exchange(jnp.broadcast_to(x[None], (n,) + x.shape), axis)


def hop(x, axis, n, step):
    return lax.ppermute(x, axis, [(i, (i + step) % n) for i in range(n)])


def last_hop(up, down, axis, n):
    pairs = []
    for i in range(n):
        for c in range(C):
            pairs.append((i * C + c, ((i + (1 if c == 0 else -1)) % n) * C + c))
    return lax.ppermute(jnp.where(lax.axis_index("c") == 0, up, down), (axis, "c"), pairs)


def block_kernel(where_ref, rows_ref, *refs):
    weights, refs = refs[:N_TENSOR], refs[N_TENSOR:]
    low_ref, out_map_ref, cot_ref, hidden_ref, sent_ref, x_buf, w_buf, acc_ref, x_sem, w_sem = refs
    parts, blocks, _, depth = x_buf.shape
    t = where_ref[0]

    def place(i):
        x, c = lax.rem(lax.div(t, C) - (0, 1, 3, 2)[i // C] + X, X), lax.rem(t + i % C, C)
        step = jnp.where(c == 0, x + 1, -x - 1)
        step = jnp.where(x == X - 1, jnp.where(c == 0, 0, 4), step)
        return lax.rem(t + step + parts, parts)

    def load(i):
        return pltpu.make_async_copy(rows_ref.at[:, place(i)], x_buf.at[i], x_sem.at[i])

    for i, weight in enumerate(weights):
        load(i).start()
        pltpu.make_async_copy(weight, w_buf.at[i], w_sem.at[i]).start()

    for i, weight in enumerate(weights):
        load(i).wait()
        pltpu.make_async_copy(weight, w_buf.at[i], w_sem.at[i]).wait()
        rows = x_buf[i].reshape(blocks * BLOCK_ROWS, depth)
        part = jnp.dot(rows, w_buf[i], preferred_element_type=F32)
        acc_ref[...] = part if i == 0 else acc_ref[...] + part

    half = cot_ref.shape[1]
    for b in range(blocks):
        rows = slice(b * BLOCK_ROWS, (b + 1) * BLOCK_ROWS)
        ranks = slice(b * RANKS, (b + 1) * RANKS)
        low = low_ref[ranks, :]
        out_map = out_map_ref[b]
        pre = acc_ref[rows, :] + lax.dot_general(
            low, out_map, (((0,), (0,)), ((), ())), preferred_element_type=F32)
        gate, up = pre[:, :half], pre[:, half:]
        sigma = jax.nn.sigmoid(gate)
        gated = gate * sigma
        hidden_ref[rows, :] = (gated * up).astype(BF16)
        live = lax.broadcasted_iota(jnp.int32, (BLOCK_ROWS, half), 0) < where_ref[1 + b]
        cotan = jnp.where(live, cot_ref[rows, :].astype(F32), 0.0)
        dgate = cotan * up * sigma * (1.0 + gate * (1.0 - sigma))
        dup = cotan * gated
        dpre = jnp.concatenate([dgate, dup], 1).astype(BF16)
        grad = jnp.dot(low, dpre, preferred_element_type=F32)
        sent_ref[:R, b * half:(b + 1) * half] = grad[:R, :half].astype(BF16)
        sent_ref[R:, b * half:(b + 1) * half] = grad[R:, half:].astype(BF16)
        dlow = lax.dot_general(out_map, dpre, (((1,), (1,)), ((), ())), preferred_element_type=F32)
        at = blocks * half + b * BLOCK_ROWS
        sent_ref[:, at:at + BLOCK_ROWS] = dlow.astype(BF16)


def project(where, rows, weights, low, out_map, cotan):
    blocks, parts, _, depth = rows.shape
    n_rows, half = cotan.shape
    any_spec = pl.BlockSpec(memory_space=pl.ANY)
    vmem_spec = pl.BlockSpec(memory_space=pltpu.VMEM)
    return pl.pallas_call(
        block_kernel,
        in_specs=[pl.BlockSpec(memory_space=pltpu.SMEM)] + [any_spec] * (1 + parts) + [vmem_spec] * 3,
        out_specs=[vmem_spec, vmem_spec],
        out_shape=[
            jax.ShapeDtypeStruct((n_rows, half), BF16),
            jax.ShapeDtypeStruct((RANKS, blocks * (half + BLOCK_ROWS)), BF16),
        ],
        scratch_shapes=[
            pltpu.VMEM((parts, blocks, BLOCK_ROWS, depth), BF16),
            pltpu.VMEM((parts,) + weights[0].shape, BF16),
            pltpu.VMEM((n_rows, 2 * half), F32),
            pltpu.SemaphoreType.DMA((parts,)),
            pltpu.SemaphoreType.DMA((parts,)),
        ],
        compiler_params=pltpu.CompilerParams(vmem_limit_bytes=VMEM_LIMIT),
        cost_estimate=pl.CostEstimate(
            flops=4 * parts * n_rows * depth * half,
            bytes_accessed=2 * parts * depth * (n_rows + 2 * half),
            transcendentals=n_rows * half),
    )(where, rows, *weights, low, out_map, cotan)


def slot_kernel(slot_ref, shared_ref, out_ref):
    blocks, _ = slot_ref.shape
    width = shared_ref.shape[1] // blocks - BLOCK_ROWS
    per = RANKS // Z
    n_out = OWN * per * N_DP
    row = lax.broadcasted_iota(jnp.int32, (n_out, N_DP), 0)
    lane = lax.broadcasted_iota(jnp.int32, (n_out, N_DP), 1)
    slot = (row & (N_DP - 1)) * OWN + lax.shift_right_logical(row, 7)
    same = (lax.shift_right_logical(row, 5) & (per - 1)) == (lane & (per - 1))
    total = None
    for b in range(blocks):
        pick = jnp.where(same & (slot == slot_ref[b:b + 1, :]), 1.0, 0.0).astype(BF16)
        term = jnp.dot(pick, shared_ref[:, b * width:(b + 1) * width], preferred_element_type=F32)
        total = term if total is None else total + term
    for i in range(OWN * per):
        out_ref[:, i * width:(i + 1) * width] = total[i * N_DP:(i + 1) * N_DP].astype(BF16)


def in_grad_kernel(mine_ref, dlow_ref, rows_ref, acc_ref, buf, sems):
    blocks, parts, _, _ = rows_ref.shape

    def load(b):
        return pltpu.make_async_copy(rows_ref.at[b], buf.at[b], sems.at[b])

    def used(b):
        return mine_ref[b] + mine_ref[blocks + b] > 0

    for b in range(blocks):
        @pl.when(used(b))
        def _():
            load(b).start()

    acc_ref[...] = jnp.zeros_like(acc_ref)
    for b in range(blocks):
        @pl.when(used(b))
        def _():
            dlow = dlow_ref[:, b * BLOCK_ROWS:(b + 1) * BLOCK_ROWS].astype(F32)
            left = jnp.concatenate(
                [jnp.where(mine_ref[s * blocks + b] > 0, dlow, 0.0) for s in range(OWN)], 0).astype(BF16)
            load(b).wait()

            for feature, step in enumerate(STEPS):
                place = lax.rem(mine_ref[OWN * blocks] + step + parts, parts)
                acc_ref[feature] += jnp.dot(left, buf[b, place], preferred_element_type=F32)


def in_grad(mine, dlow, rows):
    blocks, parts, _, depth = rows.shape
    n_out = OWN * RANKS
    vmem_spec = pl.BlockSpec(memory_space=pltpu.VMEM)
    return pl.pallas_call(
        in_grad_kernel,
        in_specs=[pl.BlockSpec(memory_space=pltpu.SMEM), vmem_spec, pl.BlockSpec(memory_space=pl.ANY)],
        out_specs=vmem_spec,
        out_shape=jax.ShapeDtypeStruct((parts, n_out, depth), F32),
        scratch_shapes=[
            pltpu.VMEM((blocks, parts, BLOCK_ROWS, depth), BF16),
            pltpu.SemaphoreType.DMA((blocks,)),
        ],
        compiler_params=pltpu.CompilerParams(vmem_limit_bytes=VMEM_LIMIT),
        cost_estimate=pl.CostEstimate(
            flops=2 * parts * n_out * blocks * BLOCK_ROWS * depth,
            bytes_accessed=2 * parts * depth * blocks * BLOCK_ROWS, transcendentals=0),
    )(mine, dlow, rows)


def by_rank(k, y):
    per = RANKS // Z
    rank = lax.broadcasted_iota(jnp.int32, (RANKS, N_DP), 0)
    source = lax.broadcasted_iota(jnp.int32, (RANKS, N_DP), 1)
    hit = (lax.shift_right_logical(rank, 2) == lax.shift_right_logical(source, 2)) & ((rank & (per - 1)) == k)
    hit = hit & ((source & (Y - 1)) == y)
    return jnp.where(hit, 1.0, 0.0).astype(BF16)


def out_grad_kernel(got_ref, out_ref):
    per = RANKS // Z
    width = out_ref.shape[2] // Y
    for y in range(Y):
        picks = [by_rank(k, y) for k in range(per)]
        for s in range(OWN):
            total = None
            for k in range(per):
                at = (s * per + k) * width
                term = jnp.dot(picks[k], got_ref[:, at:at + width], preferred_element_type=F32)
                total = term if total is None else total + term
            out_ref[s, :, y * width:(y + 1) * width] = total


def body(tokens, gate_up, adapter_in, adapter_out, d_hidden, block_adapter, block_live, owner_slot):
    dp, tensor = lax.axis_index(DP), lax.axis_index(TENSOR)
    d_part, hidden_part = tokens.shape[1], gate_up.shape[2]
    blocks = d_hidden.shape[0] // BLOCK_ROWS
    lanes = RANKS * blocks
    per = RANKS // N_TENSOR

    join = lax.optimization_barrier

    swapped = lax.ppermute(tokens, DP + TENSOR, swap(lambda z, t: (z + STEPS[t]) % Z))
    in_map = lax.dynamic_index_in_dim(adapter_in, block_adapter[dp], 0, False).reshape(RANKS, d_part)
    low_part = lax.dot_general(in_map, tokens, (((1,), (1,)), ((), ())), preferred_element_type=F32)
    low_sum = exchange(low_part.reshape(N_TENSOR, per, BLOCK_ROWS), TENSOR).sum(0).astype(BF16)
    rows = lax.all_gather(swapped, ("y", "z"), axis=0, tiled=False).reshape(Y, Z, BLOCK_ROWS, d_part)
    low_sum, gate_up, _ = join((low_sum, gate_up, swapped))

    flat = gate_up.reshape(d_part, 2 * hidden_part)
    left, right = hop(flat, "x", X, 1), hop(flat, "x", X, -1)
    own = hop(flat, "c", C, 1)
    low = spread(lax.ppermute(low_sum, DP + TENSOR, swap(lambda z, t: t)), DP, N_DP)
    left, right, own, low = join((left, right, own, low))
    far = last_hop(left, right, "x", X)
    weights = [flat, own, left, hop(left, "c", C, 1), right, hop(right, "c", C, 1), far, hop(far, "c", C, 1)]
    low = low.reshape(Z, Y, per, BLOCK_ROWS).transpose(1, 0, 2, 3).reshape(lanes, BLOCK_ROWS)

    local_ids = lax.dynamic_slice_in_dim(block_adapter, tensor * blocks, blocks, 0)
    local_live = lax.dynamic_slice_in_dim(block_live, tensor * blocks, blocks, 0)
    picked = adapter_out[local_ids]
    out_map = jnp.concatenate([
        jnp.pad(picked[:, 0], ((0, 0), (0, 0), (0, hidden_part))),
        jnp.pad(picked[:, 1], ((0, 0), (0, 0), (hidden_part, 0)))], 1)
    where = jnp.concatenate([tensor.astype(jnp.int32)[None], local_live])
    slot_of = owner_slot[block_adapter]
    local_slot = lax.dynamic_slice_in_dim(slot_of, tensor * blocks, blocks, 0)
    mine = jnp.arange(OWN, dtype=jnp.int32)[:, None] + OWN * dp == local_slot[None, :]
    slot_lane = jnp.repeat(slot_of.reshape(N_TENSOR, blocks).T, RANKS // Z, axis=1)

    hidden, sent = project(where, rows, weights, low, out_map, d_hidden)

    first = exchange(sent, "z")
    dlow = first[:, blocks * hidden_part:].astype(F32).reshape(Z, RANKS // Z, -1).sum(0).astype(BF16)
    dlow = spread(dlow, DP, N_DP).astype(F32).reshape(Z, Y, RANKS // Z, -1).sum(1).reshape(RANKS, -1)
    in_part = in_grad(jnp.append(mine.reshape(-1).astype(jnp.int32), tensor.astype(jnp.int32)), dlow, rows)
    in_part, first = join((in_part, first))
    grad_in = lax.psum_scatter(in_part, TENSOR, scatter_dimension=0, tiled=True).reshape(OWN, 2, R, d_part)
    shared = exchange(first, TENSOR)
    merged = pl.pallas_call(
        slot_kernel,
        out_shape=jax.ShapeDtypeStruct((N_DP, OWN * (RANKS // Z) * hidden_part), BF16),
    )(slot_lane, shared)
    got = exchange(merged, DP)
    grad_out = pl.pallas_call(
        out_grad_kernel,
        out_shape=jax.ShapeDtypeStruct((OWN, RANKS, Y * hidden_part), F32),
    )(got).reshape(OWN, 2, R, Y * hidden_part)
    return hidden, grad_in, grad_out


def solution(mesh):
    mesh = Mesh(mesh.devices.reshape(Z, Y, X, C), DP + TENSOR)

    return jax.shard_map(
        body,
        mesh=mesh,
        in_specs=(P(DP, TENSOR), P(TENSOR, None, DP), P(None, None, None, TENSOR), P(None, None, None, DP),
                  P(TENSOR, DP), P(), P(), P()),
        out_specs=(P(TENSOR, DP), P(DP, None, None, TENSOR), P(DP, None, None, TENSOR)),
        check_vma=False,
    )
```

```python
import jax
import jax.numpy as jnp
from jax import lax
from jax.experimental import pallas as pl
from jax.experimental.pallas import tpu as pltpu
from jax.sharding import Mesh, PartitionSpec as P

R = 16
RANKS = 2 * R
BLOCK_ROWS = 128
Z, Y, X, C = 8, 4, 4, 2
N_DP, N_TENSOR = Z * Y, X * C
OWN = 2
SLOTS = OWN * N_DP
DP, TENSOR = ("z", "y"), ("x", "c")
BF16, F32 = jnp.bfloat16, jnp.float32
VMEM_LIMIT = 48 * 2 ** 20


STEPS = (1, -1, 2, -2, 3, -3, 0, 4)


def swap(place):
    return [((z * Y + y) * N_TENSOR + t, (place(z, t) * Y + y) * N_TENSOR + z)
            for z in range(Z) for y in range(Y) for t in range(N_TENSOR)]


def exchange(x, axes):
    return lax.all_to_all(x, axes, 0, 0, tiled=True)


def spread(x, axis, n):
    return exchange(jnp.broadcast_to(x[None], (n,) + x.shape), axis)


def hop(x, axis, n, step):
    return lax.ppermute(x, axis, [(i, (i + step) % n) for i in range(n)])


def last_hop(up, down, axis, n):
    pairs = []
    for i in range(n):
        for c in range(C):
            pairs.append((i * C + c, ((i + (1 if c == 0 else -1)) % n) * C + c))
    return lax.ppermute(jnp.where(lax.axis_index("c") == 0, up, down), (axis, "c"), pairs)


def block_kernel(where_ref, rows_ref, *refs):
    weights, refs = refs[:N_TENSOR], refs[N_TENSOR:]
    low_ref, out_map_ref, cot_ref, hidden_ref, sent_ref, x_buf, w_buf, acc_ref, x_sem, w_sem = refs
    parts, blocks, _, depth = x_buf.shape
    t = where_ref[0]

    def place(i):
        x, c = lax.rem(lax.div(t, C) - (0, 1, 3, 2)[i // C] + X, X), lax.rem(t + i % C, C)
        step = jnp.where(c == 0, x + 1, -x - 1)
        step = jnp.where(x == X - 1, jnp.where(c == 0, 0, 4), step)
        return lax.rem(t + step + parts, parts)

    def load(i):
        return pltpu.make_async_copy(rows_ref.at[:, place(i)], x_buf.at[i], x_sem.at[i])

    for i, weight in enumerate(weights):
        load(i).start()
        pltpu.make_async_copy(weight, w_buf.at[i], w_sem.at[i]).start()

    for i, weight in enumerate(weights):
        load(i).wait()
        pltpu.make_async_copy(weight, w_buf.at[i], w_sem.at[i]).wait()
        rows = x_buf[i].reshape(blocks * BLOCK_ROWS, depth)
        part = jnp.dot(rows, w_buf[i], preferred_element_type=F32)
        acc_ref[...] = part if i == 0 else acc_ref[...] + part

    half = cot_ref.shape[1]
    for b in range(blocks):
        rows = slice(b * BLOCK_ROWS, (b + 1) * BLOCK_ROWS)
        ranks = slice(b * RANKS, (b + 1) * RANKS)
        low = low_ref[ranks, :]
        out_map = out_map_ref[b]
        pre = acc_ref[rows, :] + lax.dot_general(
            low, out_map, (((0,), (0,)), ((), ())), preferred_element_type=F32)
        gate, up = pre[:, :half], pre[:, half:]
        sigma = jax.nn.sigmoid(gate)
        gated = gate * sigma
        hidden_ref[rows, :] = (gated * up).astype(BF16)
        live = lax.broadcasted_iota(jnp.int32, (BLOCK_ROWS, half), 0) < where_ref[1 + b]
        cotan = jnp.where(live, cot_ref[rows, :].astype(F32), 0.0)
        dgate = cotan * up * sigma * (1.0 + gate * (1.0 - sigma))
        dup = cotan * gated
        dpre = jnp.concatenate([dgate, dup], 1).astype(BF16)
        grad = jnp.dot(low, dpre, preferred_element_type=F32)
        sent_ref[:R, b * half:(b + 1) * half] = grad[:R, :half].astype(BF16)
        sent_ref[R:, b * half:(b + 1) * half] = grad[R:, half:].astype(BF16)
        dlow = lax.dot_general(out_map, dpre, (((1,), (1,)), ((), ())), preferred_element_type=F32)
        at = blocks * half + b * BLOCK_ROWS
        sent_ref[:, at:at + BLOCK_ROWS] = dlow.astype(BF16)


def project(where, rows, weights, low, out_map, cotan):
    blocks, parts, _, depth = rows.shape
    n_rows, half = cotan.shape
    any_spec = pl.BlockSpec(memory_space=pl.ANY)
    vmem_spec = pl.BlockSpec(memory_space=pltpu.VMEM)
    return pl.pallas_call(
        block_kernel,
        in_specs=[pl.BlockSpec(memory_space=pltpu.SMEM)] + [any_spec] * (1 + parts) + [vmem_spec] * 3,
        out_specs=[vmem_spec, vmem_spec],
        out_shape=[
            jax.ShapeDtypeStruct((n_rows, half), BF16),
            jax.ShapeDtypeStruct((RANKS, blocks * (half + BLOCK_ROWS)), BF16),
        ],
        scratch_shapes=[
            pltpu.VMEM((parts, blocks, BLOCK_ROWS, depth), BF16),
            pltpu.VMEM((parts,) + weights[0].shape, BF16),
            pltpu.VMEM((n_rows, 2 * half), F32),
            pltpu.SemaphoreType.DMA((parts,)),
            pltpu.SemaphoreType.DMA((parts,)),
        ],
        compiler_params=pltpu.CompilerParams(vmem_limit_bytes=VMEM_LIMIT),
        cost_estimate=pl.CostEstimate(
            flops=4 * parts * n_rows * depth * half,
            bytes_accessed=2 * parts * depth * (n_rows + 2 * half),
            transcendentals=n_rows * half),
    )(where, rows, *weights, low, out_map, cotan)


def slot_kernel(slot_ref, shared_ref, out_ref):
    blocks, _ = slot_ref.shape
    width = out_ref.shape[1]
    per = RANKS // Z
    row = lax.broadcasted_iota(jnp.int32, (SLOTS * per, N_DP), 0)
    lane = lax.broadcasted_iota(jnp.int32, (SLOTS * per, N_DP), 1)
    slot = lax.shift_right_logical(row, 2)
    same = (row & (per - 1)) == (lane & (per - 1))
    total = None
    for b in range(blocks):
        pick = jnp.where(same & (slot == slot_ref[b:b + 1, :]), 1.0, 0.0).astype(BF16)
        term = jnp.dot(pick, shared_ref[:, b * width:(b + 1) * width], preferred_element_type=F32)
        total = term if total is None else total + term
    out_ref[...] = total.astype(BF16)


def in_grad_kernel(mine_ref, dlow_ref, rows_ref, acc_ref, buf, sems):
    blocks, parts, _, _ = rows_ref.shape

    def load(b):
        return pltpu.make_async_copy(rows_ref.at[b], buf.at[b], sems.at[b])

    def used(b):
        return mine_ref[b] + mine_ref[blocks + b] > 0

    for b in range(blocks):
        @pl.when(used(b))
        def _():
            load(b).start()

    acc_ref[...] = jnp.zeros_like(acc_ref)
    for b in range(blocks):
        @pl.when(used(b))
        def _():
            dlow = dlow_ref[:, b * BLOCK_ROWS:(b + 1) * BLOCK_ROWS].astype(F32)
            left = jnp.concatenate(
                [jnp.where(mine_ref[s * blocks + b] > 0, dlow, 0.0) for s in range(OWN)], 0).astype(BF16)
            load(b).wait()

            for feature, step in enumerate(STEPS):
                place = lax.rem(mine_ref[OWN * blocks] + step + parts, parts)
                acc_ref[feature] += jnp.dot(left, buf[b, place], preferred_element_type=F32)


def in_grad(mine, dlow, rows):
    blocks, parts, _, depth = rows.shape
    n_out = OWN * RANKS
    vmem_spec = pl.BlockSpec(memory_space=pltpu.VMEM)
    return pl.pallas_call(
        in_grad_kernel,
        in_specs=[pl.BlockSpec(memory_space=pltpu.SMEM), vmem_spec, pl.BlockSpec(memory_space=pl.ANY)],
        out_specs=vmem_spec,
        out_shape=jax.ShapeDtypeStruct((parts, n_out, depth), F32),
        scratch_shapes=[
            pltpu.VMEM((blocks, parts, BLOCK_ROWS, depth), BF16),
            pltpu.SemaphoreType.DMA((blocks,)),
        ],
        compiler_params=pltpu.CompilerParams(vmem_limit_bytes=VMEM_LIMIT),
        cost_estimate=pl.CostEstimate(
            flops=2 * parts * n_out * blocks * BLOCK_ROWS * depth,
            bytes_accessed=2 * parts * depth * blocks * BLOCK_ROWS, transcendentals=0),
    )(mine, dlow, rows)


def out_grad_kernel(got_ref, out_ref):
    rows, width = got_ref.shape
    to = lax.broadcasted_iota(jnp.int32, (rows, rows), 0)
    source = lax.broadcasted_iota(jnp.int32, (rows, rows), 1)
    shift = lax.shift_right_logical
    hit = (shift(to & 31, 2) == shift(source, 5)) & ((shift(to, 5) & 3) == (shift(source, 3) & 3))
    hit = hit & (shift(to, 7) == (shift(source, 2) & 1)) & ((to & 3) == (source & 3))
    total = jnp.dot(jnp.where(hit, 1.0, 0.0).astype(BF16), got_ref[...], preferred_element_type=F32)
    for s in range(OWN):
        for y in range(Y):
            at = (s * Y + y) * RANKS
            out_ref[s, :, y * width:(y + 1) * width] = total[at:at + RANKS]


def body(tokens, gate_up, adapter_in, adapter_out, d_hidden, block_adapter, block_live, owner_slot):
    dp, tensor = lax.axis_index(DP), lax.axis_index(TENSOR)
    d_part, hidden_part = tokens.shape[1], gate_up.shape[2]
    blocks = d_hidden.shape[0] // BLOCK_ROWS
    lanes = RANKS * blocks
    per = RANKS // N_TENSOR

    join = lax.optimization_barrier

    swapped = lax.ppermute(tokens, DP + TENSOR, swap(lambda z, t: (z + STEPS[t]) % Z))
    in_map = lax.dynamic_index_in_dim(adapter_in, block_adapter[dp], 0, False).reshape(RANKS, d_part)
    low_part = lax.dot_general(in_map, tokens, (((1,), (1,)), ((), ())), preferred_element_type=F32)
    low_sum = exchange(low_part.reshape(N_TENSOR, per, BLOCK_ROWS), TENSOR).sum(0).astype(BF16)
    rows = lax.all_gather(swapped, ("y", "z"), axis=0, tiled=False).reshape(Y, Z, BLOCK_ROWS, d_part)
    low_sum, gate_up, _ = join((low_sum, gate_up, swapped))

    flat = gate_up.reshape(d_part, 2 * hidden_part)
    left, right = hop(flat, "x", X, 1), hop(flat, "x", X, -1)
    own = hop(flat, "c", C, 1)
    low = spread(lax.ppermute(low_sum, DP + TENSOR, swap(lambda z, t: t)), DP, N_DP)
    left, right, own, low = join((left, right, own, low))
    far = last_hop(left, right, "x", X)
    weights = [flat, own, left, hop(left, "c", C, 1), right, hop(right, "c", C, 1), far, hop(far, "c", C, 1)]
    low = low.reshape(Z, Y, per, BLOCK_ROWS).transpose(1, 0, 2, 3).reshape(lanes, BLOCK_ROWS)

    local_ids = lax.dynamic_slice_in_dim(block_adapter, tensor * blocks, blocks, 0)
    local_live = lax.dynamic_slice_in_dim(block_live, tensor * blocks, blocks, 0)
    picked = adapter_out[local_ids]
    out_map = jnp.concatenate([
        jnp.pad(picked[:, 0], ((0, 0), (0, 0), (0, hidden_part))),
        jnp.pad(picked[:, 1], ((0, 0), (0, 0), (hidden_part, 0)))], 1)
    where = jnp.concatenate([tensor.astype(jnp.int32)[None], local_live])
    slot_of = owner_slot[block_adapter]
    local_slot = lax.dynamic_slice_in_dim(slot_of, tensor * blocks, blocks, 0)
    mine = jnp.arange(OWN, dtype=jnp.int32)[:, None] + OWN * dp == local_slot[None, :]
    slot_lane = jnp.repeat(slot_of.reshape(N_TENSOR, blocks).T, RANKS // Z, axis=1)

    hidden, sent = project(where, rows, weights, low, out_map, d_hidden)

    first = exchange(sent, "z")
    dlow = first[:, blocks * hidden_part:].astype(F32).reshape(Z, RANKS // Z, -1).sum(0).astype(BF16)
    dlow = spread(dlow, DP, N_DP).astype(F32).reshape(Z, Y, RANKS // Z, -1).sum(1).reshape(RANKS, -1)
    in_part = in_grad(jnp.append(mine.reshape(-1).astype(jnp.int32), tensor.astype(jnp.int32)), dlow, rows)
    in_part, first = join((in_part, first))
    grad_in = lax.psum_scatter(in_part, TENSOR, scatter_dimension=0, tiled=True).reshape(OWN, 2, R, d_part)
    shared = exchange(first, TENSOR)
    merged = pl.pallas_call(
        slot_kernel,
        out_shape=jax.ShapeDtypeStruct((SLOTS * (RANKS // Z), hidden_part), BF16),
    )(slot_lane, shared)
    got = exchange(merged, DP)
    grad_out = pl.pallas_call(
        out_grad_kernel,
        out_shape=jax.ShapeDtypeStruct((OWN, RANKS, Y * hidden_part), F32),
    )(got).reshape(OWN, 2, R, Y * hidden_part)
    return hidden, grad_in, grad_out


def solution(mesh):
    mesh = Mesh(mesh.devices.reshape(Z, Y, X, C), DP + TENSOR)

    return jax.shard_map(
        body,
        mesh=mesh,
        in_specs=(P(DP, TENSOR), P(TENSOR, None, DP), P(None, None, None, TENSOR), P(None, None, None, DP),
                  P(TENSOR, DP), P(), P(), P()),
        out_specs=(P(TENSOR, DP), P(DP, None, None, TENSOR), P(DP, None, None, TENSOR)),
        check_vma=False,
    )
```
